256 devices in a mesh: circ: 32 (over z, y_hi, core), norm: 4 (over x), span: 2 (over y_lo).
Axes of the slice: x: 4, y: 4 (y_hi: 2, y_lo: 2; y = y_hi * 2 + y_lo), z: 8, core: 2. Of those that a mesh axis runs over, the one named last changes fastest.
Arguments:
- state: float32 [5, 512, 64, 256], P(None, 'circ', 'norm', 'span'), may hold values from -6 to 6
- viscosity: float32 [512, 64, 256], P('circ', 'norm', 'span'), may hold values from 6e-05 to 0.0006
- visc_matrix: float32 [5, 5], replicated, may hold values from -2.5 to 2.5
- circ_lower_coef: float32 [512, 64, 256], P('circ', 'norm', 'span'), may hold values from 0.985 to 0.999
- circ_upper_coef: float32 [512, 64, 256], P('circ', 'norm', 'span'), may hold values from 0.985 to 0.999
- normal_lower_coef: float32 [512, 64, 256], P('circ', 'norm', 'span'), may hold values from 0.975 to 0.998
- normal_upper_coef: float32 [512, 64, 256], P('circ', 'norm', 'span'), may hold values from 0.975 to 0.998
- circ_plus: float32 [5, 5], replicated, may hold values from -0.001 to 0.992, as said below
- circ_minus: float32 [5, 5], replicated, may hold values from -0.001 to 0.992, as said below
- normal_plus: float32 [5, 5], replicated, may hold values from -0.006 to 0.975, as said below
- normal_minus: float32 [5, 5], replicated, may hold values from -0.006 to 0.975, as said below
Outputs:
- increment: float32 [5, 512, 64, 256], P(None, 'circ', 'norm', 'span')
The draws below stay inside these ranges and needn't reach their ends.
Inputs may be any that keep to these rules, and one draw needn't show every extreme that they name: `circ_plus`: diagonal entries between 0.985 and 0.992, off-diagonal entries of magnitude at most 0.001. `circ_minus`: diagonal entries between 0.985 and 0.992, off-diagonal entries of magnitude at most 0.001. `normal_plus`: diagonal entries between 0.95 and 0.975, off-diagonal entries of magnitude at most 0.006. `normal_minus`: diagonal entries between 0.95 and 0.975, off-diagonal entries of magnitude at most 0.006.
All inputs are finite; a program needn't handle non-finite values.
Results may differ from the reference program's by a relative error of at most 0.0003.
Values sent between devices are 32-bit elements; how exact they have to be, the bound alone decides.
A program may use at most 64 MiB of HBM per device.

```python
import math
import jax
import jax.numpy as jnp
from jax import lax

NVARS = 5
NC = 512
NN = 64
NS = 256


def split_jacobian(key, size, diag_low, diag_high, off_size):
    diag_key, off_key = jax.random.split(key)
    diag = jax.random.uniform(diag_key, (size,), jnp.float32, diag_low, diag_high)
    off = jax.random.uniform(off_key, (size, size), jnp.float32, -off_size, off_size)
    eye = jnp.eye(size, dtype=jnp.float32)
    return off * (1.0 - eye) + eye * diag[None, :]


def draw_circ_plus(key, part):
    key = jax.random.fold_in(key, 11)
    return split_jacobian(key, NVARS, 0.985, 0.992, 0.001)


def draw_circ_minus(key, part):
    key = jax.random.fold_in(key, 12)
    return split_jacobian(key, NVARS, 0.985, 0.992, 0.001)


def draw_normal_plus(key, part):
    key = jax.random.fold_in(key, 13)
    return split_jacobian(key, NVARS, 0.95, 0.975, 0.006)


def draw_normal_minus(key, part):
    key = jax.random.fold_in(key, 14)
    return split_jacobian(key, NVARS, 0.95, 0.975, 0.006)


def level_of(key, shape, shards, low, largest):
    level, own = 1.0, jax.random.fold_in(key, 6)
    for position, shards_of in shards:
        steps = jnp.exp(jax.random.uniform(jax.random.fold_in(own, position), (shards_of,), jnp.float32, low / len(shards), largest / len(shards)))
        level = level * jnp.repeat(steps, shape[position] // shards_of).reshape([-1 if axis == position else 1 for axis in range(len(shape))])
    return level


def centred(stream_key, dims, width, bound, cuts=(), kind=jnp.bfloat16):
    values = jax.random.normal(stream_key, dims, jnp.float32) * width
    if len(cuts) > 0:
        values = level_of(stream_key, dims, cuts, -0.22, 0.18) * values
    return jnp.clip(values, min=-bound, max=bound).astype(kind)


def setup_inputs(seed: int = 0) -> dict:
    keys = jax.random.split(jax.random.key(seed), 12)
    state = centred(keys[0], (NVARS, NC, NN, NS), 1.0, 6.0, ((1, 32), (2, 4), (3, 2)), jnp.float32)
    viscosity = jnp.clip(jnp.exp(math.log(0.0006) - 2.3025852 * jax.random.uniform(keys[1], (NC, NN, NS), jnp.float32) ** level_of(keys[1], (NC, NN, NS), ((0, 32), (1, 4), (2, 2)), -0.2, 0.2)), 5.999999848427251e-05, 0.0006)
    visc_matrix = centred(keys[2], (NVARS, NVARS), NVARS ** -0.5, 2.5, (), jnp.float32)
    circ_lower_coef = jnp.clip(jnp.exp(math.log(0.999) - 0.014113136 * jax.random.uniform(keys[3], (NC, NN, NS), jnp.float32) ** level_of(keys[3], (NC, NN, NS), ((0, 32), (1, 4), (2, 2)), -0.2, 0.2)), 0.985, 0.999)
    circ_upper_coef = jnp.clip(jnp.exp(math.log(0.999) - 0.014113136 * jax.random.uniform(keys[4], (NC, NN, NS), jnp.float32) ** level_of(keys[4], (NC, NN, NS), ((0, 32), (1, 4), (2, 2)), -0.2, 0.2)), 0.985, 0.999)
    normal_lower_coef = jnp.clip(jnp.exp(math.log(0.998) - 0.0233158067 * jax.random.uniform(keys[5], (NC, NN, NS), jnp.float32) ** level_of(keys[5], (NC, NN, NS), ((0, 32), (1, 4), (2, 2)), -0.2, 0.2)), 0.975, 0.998)
    normal_upper_coef = jnp.clip(jnp.exp(math.log(0.998) - 0.0233158067 * jax.random.uniform(keys[6], (NC, NN, NS), jnp.float32) ** level_of(keys[6], (NC, NN, NS), ((0, 32), (1, 4), (2, 2)), -0.2, 0.2)), 0.975, 0.998)
    circ_plus = draw_circ_plus(jax.random.fold_in(keys[11], 71), 0)
    circ_minus = draw_circ_minus(jax.random.fold_in(keys[11], 71), 0)
    normal_plus = draw_normal_plus(jax.random.fold_in(keys[11], 71), 0)
    normal_minus = draw_normal_minus(jax.random.fold_in(keys[11], 71), 0)
    return dict(state=state, viscosity=viscosity, visc_matrix=visc_matrix, circ_lower_coef=circ_lower_coef, circ_upper_coef=circ_upper_coef, normal_lower_coef=normal_lower_coef, normal_upper_coef=normal_upper_coef, circ_plus=circ_plus, circ_minus=circ_minus, normal_plus=normal_plus, normal_minus=normal_minus)


def apply_matrix(mat, vec):
    return jnp.einsum('ab,bxy->axy', mat, vec, precision=lax.Precision.HIGHEST)


def power_of(mat, count):
    result = jnp.eye(mat.shape[0], dtype=jnp.float32)
    base = mat
    while count > 0:
        if count % 2 == 1:
            result = jnp.dot(result, base, precision=lax.Precision.HIGHEST)
        base = jnp.dot(base, base, precision=lax.Precision.HIGHEST)
        count = count // 2
    return result


def solve_five(scale, jmat, vec):
    size = jmat.shape[0]
    rows = [[(1.0 if r == c else 0.0) - scale * jmat[r, c] for c in range(size)] for r in range(size)]
    right = [vec[r] for r in range(size)]
    for k in range(size):
        for r in range(k + 1, size):
            factor = rows[r][k] / rows[k][k]
            for c in range(k + 1, size):
                rows[r][c] = rows[r][c] - factor * rows[k][c]
            right[r] = right[r] - factor * right[k]
    result = [None] * size
    for r in range(size - 1, -1, -1):
        total = right[r]
        for c in range(r + 1, size):
            total = total - rows[r][c] * result[c]
        result[r] = total / rows[r][r]
    return jnp.stack(result, 0)


def sweep(field, coef, mat, start, axis, backward):
    items = (jnp.moveaxis(field, axis, 0), jnp.moveaxis(coef, axis - 1, 0))

    def step(carry, item):
        value, scale = item
        carry = value + scale[None] * apply_matrix(mat, carry)
        return carry, carry

    last, values = lax.scan(step, start, items, reverse=backward)
    return jnp.moveaxis(values, 0, axis), last


def periodic_sweep(field, coef, mat, backward):
    zero = jnp.zeros((field.shape[0], field.shape[2], field.shape[3]), jnp.float32)
    _, last = sweep(field, coef, mat, zero, 1, backward)
    closing = solve_five(jnp.prod(coef, axis=0), power_of(mat, field.shape[1]), last)
    values, _ = sweep(field, coef, mat, closing, 1, backward)
    return values


def reference(state, viscosity, visc_matrix, circ_lower_coef, circ_upper_coef, normal_lower_coef, normal_upper_coef, circ_plus, circ_minus, normal_plus, normal_minus):
    beside_all = jnp.roll(state, 1, 1) + jnp.roll(state, -1, 1)
    across = jnp.roll(state, 1, 3) + jnp.roll(state, -1, 3)
    padded = jnp.pad(state, ((0, 0), (0, 0), (1, 1), (0, 0)))
    outward = padded[:, :, 2:] + padded[:, :, :-2]
    lap = beside_all + across + outward - 6.0 * state
    rhs = viscosity[None] * apply_matrix(visc_matrix, lap.reshape(lap.shape[0], lap.shape[1], -1)).reshape(lap.shape)
    lower_circ = periodic_sweep(rhs, circ_lower_coef, circ_plus, False)
    upper_circ = periodic_sweep(lower_circ, circ_upper_coef, circ_minus, True)
    zero = jnp.zeros((state.shape[0], state.shape[1], state.shape[3]), jnp.float32)
    lower_normal, _ = sweep(upper_circ, normal_lower_coef, normal_plus, zero, 2, False)
    increment, _ = sweep(lower_normal, normal_upper_coef, normal_minus, zero, 2, True)
    return increment
```

```python
import jax
import jax.numpy as jnp
from jax import lax
from jax.experimental import pallas as pl
from jax.experimental.pallas import tpu as pltpu
from jax.sharding import PartitionSpec as P

MESH = pl.DeviceIdType.MESH
NV = 5
CIRC, NORM = 32, 4
STEPS = 16
LANES = 128
OWNERS = 16
STEP_UNROLL = 2


def place(seg):
    return lax.rem(seg, 4) * 8 + seg // 4


def shifted(groups, d, reverse):
    def turn(x, k):
        return pltpu.roll(x, 8 - k if reverse else k, axis=0)

    if d >= 4:
        return [turn(x, d // 4) for x in groups]
    if reverse:
        return [groups[v + d] if v + d < 4 else turn(groups[v + d - 4], 1) for v in range(4)]
    return [groups[v - d] if v >= d else turn(groups[v - d + 4], 1) for v in range(4)]


def apply(mat, vec):
    out = []
    for r in range(NV):
        total = mat[r][0] * vec[0]
        for c in range(1, NV):
            total = total + mat[r][c] * vec[c]
        out.append(total)
    return out


def matmul(a, b):
    out = []
    for r in range(NV):
        for c in range(NV):
            total = a[NV * r] * b[c]
            for k in range(1, NV):
                total = total + a[NV * r + k] * b[NV * k + c]
            out.append(total)
    return out


def inverse(scale, mat):
    rows = [
        [(1.0 if r == c else 0.0) - scale * mat[r][c] for c in range(NV)] for r in range(NV)
    ]
    inv = [[None] * NV for _ in range(NV)]
    for k in range(NV):
        pivot = 1.0 / rows[k][k]
        for c in range(NV):
            rows[k][c] = pivot if c == k else rows[k][c] * pivot
        for r in range(NV):
            if r == k:
                continue
            factor = rows[r][k]
            for c in range(NV):
                if c == k:
                    rows[r][c] = -factor * pivot
                else:
                    rows[r][c] = rows[r][c] - factor * rows[k][c]
    return rows


def scalars(ref):
    return [[ref[r, c] for c in range(NV)] for r in range(NV)]


def steps(body, start, reverse=False):
    def several(t, carry):
        for u in range(STEP_UNROLL):
            i = t * STEP_UNROLL + u
            carry = body(STEPS - 1 - i if reverse else i, carry)
        return carry

    return lax.fori_loop(0, STEPS // STEP_UNROLL, several, start)


def each(count, body):
    def one(k, carry):
        body(k)
        return carry

    lax.fori_loop(0, count, one, 0)


def kernel(
    state, visc_in, cl_in, cu_in, nl_in, nu_in, vm_in, cp_in, cm_in, np_in, nm_in,
    out,
    field, visc, cl, cu, nl, nu, rhs, low, turned, low_t,
    edge, edge_in, w_own, b_own, w_all, b_all, back, back_in,
    power, k_circ, k_norm, level, r_circ, a_low, a_up, g_low, g_up, m_norm, w_norm, rn, bn,
    load_sem, tl_sem, tu_sem, self_sem,
    halo_send, halo_recv, w_send, w_recv, b_send, b_recv, p_send, p_recv,
    rn_send, rn_recv, bl_send, bl_recv, bu_send, bu_recv,
):
    c, n, s = lax.axis_index("circ"), lax.axis_index("norm"), lax.axis_index("span")
    owner = lax.rem(c, 2) == 0
    row = c // 2
    zero = jnp.zeros((STEPS, LANES), jnp.float32)
    one = jnp.ones((STEPS, LANES), jnp.float32)

    def remote(src, dst, send, recv, to):
        return pltpu.make_async_remote_copy(
            src_ref=src, dst_ref=dst, send_sem=send, recv_sem=recv, device_id=to, device_id_type=MESH
        )

    barrier = pltpu.get_barrier_semaphore()

    def greet(d):
        to = lax.rem(c + d + 1, CIRC)

        @pl.when(jnp.logical_or(owner, lax.rem(to, 2) == 0))
        def _():
            pl.semaphore_signal(barrier, inc=1, device_id=(to, n, s), device_id_type=MESH)

    each(CIRC - 1, greet)
    for d in range(1, NORM):
        pl.semaphore_signal(
            barrier, inc=1, device_id=(c, lax.rem(n + d, NORM), s), device_id_type=MESH
        )
    pl.semaphore_signal(barrier, inc=1, device_id=(c, n, 1 - s), device_id_type=MESH)

    inside = pltpu.make_async_copy(
        state, field.at[:, pl.ds(1, STEPS), pl.ds(0, STEPS)], load_sem.at[0]
    )
    loads = [
        pltpu.make_async_copy(src, dst, load_sem.at[1 + k])
        for k, (src, dst) in enumerate(((cl_in, cl), (cu_in, cu), (visc_in, visc)))
    ]
    inside.start()
    for copy in loads:
        copy.start()

    def turn(src, dst, sem, j):
        return pltpu.make_async_copy(src.at[:, j], dst.at[j], sem.at[j])

    def fetch(j):
        turn(nl_in, nl, tl_sem, j).start()
        turn(nu_in, nu, tu_sem, j).start()

    each(STEPS, fetch)

    lane8 = lax.broadcasted_iota(jnp.int32, (8, LANES), 1)
    sub8 = lax.broadcasted_iota(jnp.int32, (8, LANES), 0)
    group = lane8 // 32
    base = []
    for r in range(NV):
        for k in range(NV):
            base.append(
                jnp.where(
                    group == 0,
                    cp_in[r, k],
                    jnp.where(group == 1, cm_in[r, k], jnp.where(group == 2, np_in[r, k], nm_in[r, k])),
                )
            )

    def square(t, mat):
        for e in range(NV * NV):
            power[t, e] = mat[e]
        return tuple(matmul(mat, mat))

    last = lax.fori_loop(0, 9, square, tuple(base))
    for e in range(NV * NV):
        power[9, e] = last[e]

    def kept(t):
        return [power[t, e] for e in range(NV * NV)]

    run = [
        jnp.where(sub8 % 2 == 1, base[e], 1.0 if e % (NV + 1) == 0 else 0.0) for e in range(NV * NV)
    ]
    for bit in (1, 2):
        more = matmul(run, kept(bit))
        run = [jnp.where((sub8 // (1 << bit)) % 2 == 1, more[e], run[e]) for e in range(NV * NV)]
    for half in range(2):
        if half == 1:
            run = matmul(run, kept(3))
        ahead = matmul(run, kept(0))
        both = matmul(run, [pltpu.roll(x, 32, axis=1) for x in ahead])
        for e in range(NV * NV):
            k_circ[e, pl.ds(8 * half, 8)] = jnp.broadcast_to(both[e][:, 32:33], (8, LANES))
            k_norm[e, pl.ds(8 * half, 8)] = jnp.broadcast_to(both[e][:, 96:97], (8, LANES))

    def spread(t, carry):
        for e in range(NV * NV):
            mat = power[4 + t, e]
            level[t, e] = jnp.broadcast_to(mat[:, 0:1], (8, LANES))
            level[6 + t, e] = jnp.broadcast_to(mat[:, 32:33], (8, LANES))
        return carry

    lax.fori_loop(0, 6, spread, 0)
    for e in range(NV * NV):
        m_norm[0, e] = jnp.broadcast_to(power[4, e][:, 64:65], (8, LANES))
        m_norm[1, e] = jnp.broadcast_to(power[4, e][:, 96:97], (8, LANES))

    def responses(weight, count, table, store):
        for v in range(count):
            w = [weight(i, v) for i in range(STEPS)]
            for e in range(NV * NV):
                total = w[0] * table[e, pl.ds(0, 1)]
                for i in range(1, STEPS):
                    total = total + w[i] * table[e, pl.ds(i, 1)]
                store(e, v, total)

    for copy in loads:
        copy.wait()

    def circ_scales(i, carry):
        p, q = carry
        p = p * cl[i]
        w_own[2 + i] = q * p
        return p, q * cu[i]

    p, q = steps(circ_scales, (one, one))
    w_own[0] = p
    w_own[1] = q

    inside.wait()
    lane = lax.broadcasted_iota(jnp.int32, (STEPS, LANES), 1)

    def slot(a, i):
        return (0, a * STEPS + i) if a < 4 else (1, i)

    def pack(i, packs):
        packs = list(packs)
        for a in range(NV):
            g, k = slot(a, i)
            mine = lax.rem(lane - 2 * k + 1 + LANES, LANES) <= 1
            moved = pltpu.roll(field[a, i + 1, pl.ds(0, STEPS)], 2 * k, axis=1)
            packs[g] = jnp.where(mine, moved, packs[g])
        return tuple(packs)

    packs = steps(pack, (zero, zero))
    for g in range(2):
        edge[g] = jnp.where(lane % 2 == 1, pltpu.roll(packs[g], 2, axis=1), packs[g])

    pl.semaphore_wait(barrier, jnp.where(owner, CIRC - 1, OWNERS) + NORM)

    to_next = remote(
        field.at[:, STEPS, pl.ds(0, STEPS)], field.at[:, 0, pl.ds(0, STEPS)],
        halo_send.at[0], halo_recv.at[0], (lax.rem(c + 1, CIRC), n, s),
    )
    to_prev = remote(
        field.at[:, 1, pl.ds(0, STEPS)], field.at[:, STEPS + 1, pl.ds(0, STEPS)],
        halo_send.at[1], halo_recv.at[1], (lax.rem(c + CIRC - 1, CIRC), n, s),
    )
    to_side = remote(edge, edge_in, halo_send.at[2], halo_recv.at[2], (c, n, 1 - s))
    to_up = remote(
        field.at[:, pl.ds(1, STEPS), STEPS - 1], field.at[:, pl.ds(1, STEPS), 23],
        halo_send.at[3], halo_recv.at[3], (c, n + 1, s),
    )
    to_down = remote(
        field.at[:, pl.ds(1, STEPS), 0], field.at[:, pl.ds(1, STEPS), STEPS],
        halo_send.at[4], halo_recv.at[4], (c, n - 1, s),
    )
    has_up, has_down = n < NORM - 1, n > 0
    to_next.start()
    to_prev.start()
    to_side.start()
    pl.when(has_up)(to_up.start)
    pl.when(has_down)(to_down.start)

    def nothing_at(at):
        def fill(i, carry):
            for a in range(NV):
                field[a, i + 1, pl.ds(at, 1)] = jnp.zeros((1, LANES), jnp.float32)
            return carry

        steps(fill, 0)

    pl.when(jnp.logical_not(has_up))(lambda: nothing_at(STEPS))
    pl.when(jnp.logical_not(has_down))(lambda: nothing_at(23))

    def to_owner(src, dst, send, recv, j):
        return remote(
            src.at[:, j], dst.at[:, place(c)], send.at[j], recv.at[c], (2 * j, n, s)
        )

    def from_segment(src, dst, send, recv, k):
        return remote(src.at[:, 0], dst.at[:, place(k)], send.at[0], recv.at[k], (c, n, s))

    def hand_in(src, dst, send, recv, k):
        def one_row(j):
            @pl.when(2 * j != c)
            def _():
                to_owner(src, dst, send, recv, j).start()

        each(OWNERS, one_row)

        @pl.when(owner)
        def _():
            pltpu.make_async_copy(src.at[:, row], dst.at[:, place(c)], self_sem.at[k]).start()

    def collected(src, dst, send, recv, k):
        def one_segment(seg):
            @pl.when(seg != c)
            def _():
                from_segment(src, dst, send, recv, seg).wait_recv()

        each(CIRC, one_segment)
        pltpu.make_async_copy(src.at[:, row], dst.at[:, place(c)], self_sem.at[k]).wait()

    hand_in(w_own, w_all, w_send, w_recv, 0)

    def fetched(j):
        turn(nl_in, nl, tl_sem, j).wait()
        turn(nu_in, nu, tu_sem, j).wait()

    each(STEPS, fetched)

    def norm_scales(j, carry):
        p, q = carry
        p = p * nl[j]
        w_norm[j] = q * p
        return p, q * nu[j]

    p, q = steps(norm_scales, (one, one))
    rn[n, 0] = p
    rn[n, 1] = q

    def keep_norm(e, v, total):
        rn[n, 2 + e, pl.ds(8 * v, 8)] = total

    responses(lambda j, v: w_norm[j, pl.ds(8 * v, 8)], 2, k_norm, keep_norm)

    def over_norm(d, buf, send, recv):
        to = lax.rem(n + d, NORM)
        return remote(buf.at[n], buf.at[n], send.at[d], recv.at[n], (c, to, s))

    def from_norm(d, buf, send, recv):
        k = lax.rem(n + d, NORM)
        return remote(buf.at[k], buf.at[k], send.at[d], recv.at[k], (c, k, s))

    for d in range(1, NORM):
        over_norm(d, rn, rn_send, rn_recv).start()

    to_next.wait_recv()
    to_prev.wait_recv()
    to_side.wait_recv()
    pl.when(has_up)(to_down.wait_recv)
    pl.when(has_down)(to_up.wait_recv)

    vm, cp, cm = scalars(vm_in), scalars(cp_in), scalars(cm_in)

    def sweep_step(value, scale, mat, carry):
        moved = apply(mat, carry)
        return tuple(value[a] + scale * moved[a] for a in range(NV))

    def first_low(i, carry):
        lap = []
        for a in range(NV):
            tall = field[a, i + 1]
            mid = tall[:STEPS]
            wall = pltpu.roll(tall, 1, axis=0)[:STEPS] + pltpu.roll(tall, 23, axis=0)[:STEPS]
            g, k = slot(a, i)
            beyond = pltpu.roll(edge_in[g], LANES - 1 - 2 * k, axis=1)
            left = jnp.where(lane == 0, beyond, pltpu.roll(mid, 1, axis=1))
            right = jnp.where(lane == LANES - 1, beyond, pltpu.roll(mid, LANES - 1, axis=1))
            around = field[a, i, pl.ds(0, STEPS)] + field[a, i + 2, pl.ds(0, STEPS)]
            lap.append(around + (left + right) + wall - 6.0 * mid)
        mixed = apply(vm, lap)
        value = [visc[i] * x for x in mixed]
        for a in range(NV):
            rhs[a, i] = value[a]
        carry = sweep_step(value, cl[i], cp, carry)
        for a in range(NV):
            low[a, i] = carry[a]
        return carry

    zeros = (zero,) * NV
    end = steps(first_low, zeros)
    for a in range(NV):
        b_own[a] = end[a]

    def first_up(i, carry):
        return sweep_step([low[a, i] for a in range(NV)], cu[i], cm, carry)

    end = steps(first_up, zeros, reverse=True)
    for a in range(NV):
        b_own[NV + a] = end[a]
    hand_in(b_own, b_all, b_send, b_recv, 1)

    def quad(ref, *at):
        return [ref[(*at, pl.ds(8 * v, 8))] for v in range(4)]

    def table(ref, *at):
        return [[ref[(*at, NV * r + k)] for k in range(NV)] for r in range(NV)]

    def to_segment(k):
        return remote(
            back.at[:, place(k)], back_in.at[:, row], p_send.at[k], p_recv.at[row], (k, n, s)
        )

    def from_owner(j):
        return remote(back.at[:, 0], back_in.at[:, j], p_send.at[0], p_recv.at[j], (2 * j, n, s))

    @pl.when(owner)
    def _():
        collected(w_own, w_all, w_send, w_recv, 0)

        def keep_circ(e, v, total):
            r_circ[e, pl.ds(8 * v, 8)] = total

        responses(lambda i, v: w_all[2 + i, pl.ds(8 * v, 8)], 4, k_circ, keep_circ)
        for side, (store, inv) in enumerate(((a_low, g_low), (a_up, g_up))):
            scale = quad(w_all, side)
            for t in range(5):
                for v in range(4):
                    store[t, pl.ds(8 * v, 8)] = scale[v]
                beside = shifted(scale, 1 << t, side == 1)
                scale = [scale[v] * beside[v] for v in range(4)]
            solved = inverse(scale[0], table(level, 6 * side + 5))
            for r in range(NV):
                for k in range(NV):
                    inv[NV * r + k] = solved[r][k]

        collected(b_own, b_all, b_send, b_recv, 1)

        def closed(shift, side, store, inv):
            for t in range(5):
                beside = [shifted(x, 1 << t, side == 1) for x in shift]
                scale = quad(store, t)
                mat = table(level, 6 * side + t)
                moved = [apply(mat, [beside[a][v] for a in range(NV)]) for v in range(4)]
                shift = [
                    [shift[a][v] + scale[v] * moved[v][a] for v in range(4)] for a in range(NV)
                ]
            mat = table(inv)
            solved = [apply(mat, [shift[a][v] for a in range(NV)]) for v in range(4)]
            return [shifted([solved[v][a] for v in range(4)], 1, side == 1) for a in range(NV)]

        enter = closed([quad(b_all, a) for a in range(NV)], 0, a_low, g_low)
        for a in range(NV):
            for v in range(4):
                back[a, pl.ds(8 * v, 8)] = enter[a][v]
        shift = [quad(b_all, NV + a) for a in range(NV)]
        for r in range(NV):
            for k in range(NV):
                response = quad(r_circ, NV * r + k)
                shift[r] = [shift[r][v] + response[v] * enter[k][v] for v in range(4)]
        enter = closed(shift, 1, a_up, g_up)
        for a in range(NV):
            for v in range(4):
                back[NV + a, pl.ds(8 * v, 8)] = enter[a][v]

        def give(k):
            @pl.when(k != c)
            def _():
                to_segment(k).start()

        each(CIRC, give)
        own = pltpu.make_async_copy(back.at[:, place(c)], back_in.at[:, row], self_sem.at[2])
        own.start()
        own.wait()

    def given(j):
        @pl.when(2 * j != c)
        def _():
            from_owner(j).wait_recv()

    each(OWNERS, given)

    def second_low(i, carry):
        carry = sweep_step([rhs[a, i] for a in range(NV)], cl[i], cp, carry)
        for a in range(NV):
            low[a, i] = carry[a]
        return carry

    steps(second_low, tuple(back_in[a] for a in range(NV)))

    def second_up(i, carry):
        carry = sweep_step([low[a, i] for a in range(NV)], cu[i], cm, carry)
        for a in range(NV):
            turned[a, pl.ds(i, STEPS, stride=STEPS)] = carry[a]
        return carry

    steps(second_up, tuple(back_in[NV + a] for a in range(NV)), reverse=True)

    nplus, nminus = scalars(np_in), scalars(nm_in)

    def across(j):
        return [turned[a, pl.ds(pl.multiple_of(j * STEPS, STEPS), STEPS)] for a in range(NV)]

    def norm_low(j, carry):
        carry = sweep_step(across(j), nl[j], nplus, carry)
        for a in range(NV):
            low_t[a, j] = carry[a]
        return carry

    def norm_up(j, carry):
        return sweep_step([low_t[a, j] for a in range(NV)], nu[j], nminus, carry)

    bl, bu = bn.at[0], bn.at[1]
    end = steps(norm_low, zeros)
    for a in range(NV):
        bn[0, n, a] = end[a]
    for d in range(1, NORM):
        @pl.when(n < NORM - 1)
        def _():
            over_norm(d, bl, bl_send, bl_recv).start()

    end = steps(norm_up, zeros, reverse=True)
    for a in range(NV):
        bn[1, n, a] = end[a]
    for d in range(1, NORM):
        @pl.when(lax.rem(n + d, NORM) < n)
        def _():
            over_norm(d, bu, bu_send, bu_recv).start()

    for d in range(1, NORM):
        k = lax.rem(n + d, NORM)
        from_norm(d, rn, rn_send, rn_recv).wait_recv()
        pl.when(k < NORM - 1)(from_norm(d, bl, bl_send, bl_recv).wait_recv)
        pl.when(k > n)(from_norm(d, bu, bu_send, bu_recv).wait_recv)

    def entering(v):
        half = pl.ds(8 * v, 8)
        plus, minus = table(m_norm, 0), table(m_norm, 1)
        x = {1: [bn[0, 0, a, half] for a in range(NV)]}
        for k in (1, 2):
            moved = apply(plus, x[k])
            x[k + 1] = [bn[0, k, a, half] + rn[k, 0, half] * moved[a] for a in range(NV)]
        y = {}
        for k in (3, 2, 1):
            value = [bn[1, k, a, half] for a in range(NV)]
            for r in range(NV):
                for a in range(NV):
                    value[r] = value[r] + rn[k, 2 + NV * r + a, half] * x[k][a]
            if k < 3:
                moved = apply(minus, y[k])
                value = [value[a] + rn[k, 1, half] * moved[a] for a in range(NV)]
            y[k - 1] = value
        none = jnp.zeros((8, LANES), jnp.float32)
        low_in, up_in = [none] * NV, [none] * NV
        for k in (1, 2, 3):
            low_in = [jnp.where(n == k, x[k][a], low_in[a]) for a in range(NV)]
            up_in = [jnp.where(n == k - 1, y[k - 1][a], up_in[a]) for a in range(NV)]
        return low_in, up_in

    halves = [entering(v) for v in range(2)]
    starts = [
        tuple(jnp.concatenate([halves[0][side][a], halves[1][side][a]], axis=0) for a in range(NV))
        for side in range(2)
    ]
    steps(norm_low, starts[0])

    def last_up(j, carry):
        carry = norm_up(j, carry)
        for a in range(NV):
            out[a, pl.ds(j, STEPS, stride=STEPS)] = carry[a]
        return carry

    steps(last_up, starts[1], reverse=True)

    to_next.wait_send()
    to_prev.wait_send()
    to_side.wait_send()
    pl.when(has_up)(to_up.wait_send)
    pl.when(has_down)(to_down.wait_send)

    def sent(j):
        @pl.when(2 * j != c)
        def _():
            to_owner(w_own, w_all, w_send, w_recv, j).wait_send()
            to_owner(b_own, b_all, b_send, b_recv, j).wait_send()

    each(OWNERS, sent)

    @pl.when(owner)
    def _():
        def returned(k):
            @pl.when(k != c)
            def _():
                to_segment(k).wait_send()

        each(CIRC, returned)

    for d in range(1, NORM):
        over_norm(d, rn, rn_send, rn_recv).wait_send()
        pl.when(n < NORM - 1)(over_norm(d, bl, bl_send, bl_recv).wait_send)
        pl.when(lax.rem(n + d, NORM) < n)(over_norm(d, bu, bu_send, bu_recv).wait_send)


def per_device(
    state, viscosity, visc_matrix, circ_lower_coef, circ_upper_coef, normal_lower_coef,
    normal_upper_coef, circ_plus, circ_minus, normal_plus, normal_minus,
):
    f32 = jnp.float32

    def vmem(*shape):
        return pltpu.VMEM(shape, f32)

    plane = (STEPS, LANES)
    block = (STEPS, STEPS, LANES)
    mats = NV * NV
    dma = pltpu.SemaphoreType.DMA
    scratch = [
        vmem(NV, STEPS + 2, 24, LANES),
        *[vmem(*block) for _ in range(5)],
        vmem(NV, *block), vmem(NV, *block),
        vmem(NV, STEPS * STEPS, LANES), vmem(NV, *block),
        vmem(2, *plane), vmem(2, *plane),
        vmem(18, *plane), vmem(2 * NV, *plane),
        vmem(18, CIRC, LANES), vmem(2 * NV, CIRC, LANES),
        vmem(2 * NV, CIRC, LANES), vmem(2 * NV, *plane),
        vmem(10, mats, 8, LANES),
        vmem(mats, *plane), vmem(mats, *plane),
        vmem(12, mats, 8, LANES), vmem(mats, CIRC, LANES),
        vmem(5, CIRC, LANES), vmem(5, CIRC, LANES),
        vmem(mats, 8, LANES), vmem(mats, 8, LANES), vmem(2, mats, 8, LANES),
        vmem(*block), vmem(NORM, mats + 2, *plane), vmem(2, NORM, NV, *plane),
        dma((4,)), dma((STEPS,)), dma((STEPS,)), dma((3,)),
        dma((5,)), dma((5,)),
        dma((OWNERS,)), dma((CIRC,)), dma((OWNERS,)), dma((CIRC,)),
        dma((CIRC,)), dma((OWNERS,)),
        *[dma((NORM,)) for _ in range(6)],
    ]
    anywhere = pl.BlockSpec(memory_space=pl.ANY)
    small = pl.BlockSpec(memory_space=pltpu.SMEM)
    flat = pl.pallas_call(
        kernel,
        out_shape=jax.ShapeDtypeStruct((NV, STEPS * STEPS, LANES), f32),
        in_specs=[anywhere] * 6 + [small] * 5,
        out_specs=pl.BlockSpec(memory_space=pltpu.VMEM),
        scratch_shapes=scratch,
        compiler_params=pltpu.CompilerParams(
            collective_id=0, has_side_effects=True, vmem_limit_bytes=32 * 1024 * 1024
        ),
    )(
        state, viscosity, circ_lower_coef, circ_upper_coef, normal_lower_coef, normal_upper_coef,
        visc_matrix, circ_plus, circ_minus, normal_plus, normal_minus,
    )
    return flat.reshape(NV, STEPS, STEPS, LANES)


def solution(mesh):
    placed = (
        P(None, "circ", "norm", "span"),
        P("circ", "norm", "span"),
        P(),
        P("circ", "norm", "span"),
        P("circ", "norm", "span"),
        P("circ", "norm", "span"),
        P("circ", "norm", "span"),
        P(),
        P(),
        P(),
        P(),
    )
    return jax.shard_map(
        per_device,
        mesh=mesh,
        in_specs=placed,
        out_specs=P(None, "circ", "norm", "span"),
        check_vma=False,
    )
```

```python
import jax
import jax.numpy as jnp
from jax import lax
from jax.experimental import pallas as pl
from jax.experimental.pallas import tpu as pltpu
from jax.sharding import PartitionSpec as P

MESH = pl.DeviceIdType.MESH
NV = 5
CIRC, NORM = 32, 4
STEPS = 16
LANES = 128
OWNERS = 16
STEP_UNROLL = 8
SEND_UNROLL = 2


def place(seg):
    return lax.rem(seg, 4) * 8 + seg // 4


def shifted(groups, d, reverse):
    def turn(x, k):
        return pltpu.roll(x, 8 - k if reverse else k, axis=0)

    if d >= 4:
        return [turn(x, d // 4) for x in groups]
    if reverse:
        return [groups[v + d] if v + d < 4 else turn(groups[v + d - 4], 1) for v in range(4)]
    return [groups[v - d] if v >= d else turn(groups[v - d + 4], 1) for v in range(4)]


def apply(mat, vec):
    out = []
    for r in range(NV):
        total = mat[r][0] * vec[0]
        for c in range(1, NV):
            total = total + mat[r][c] * vec[c]
        out.append(total)
    return out


def matmul(a, b):
    out = []
    for r in range(NV):
        for c in range(NV):
            total = a[NV * r] * b[c]
            for k in range(1, NV):
                total = total + a[NV * r + k] * b[NV * k + c]
            out.append(total)
    return out


def inverse(scale, mat):
    rows = [
        [(1.0 if r == c else 0.0) - scale * mat[r][c] for c in range(NV)] for r in range(NV)
    ]
    inv = [[None] * NV for _ in range(NV)]
    for k in range(NV):
        pivot = 1.0 / rows[k][k]
        for c in range(NV):
            rows[k][c] = pivot if c == k else rows[k][c] * pivot
        for r in range(NV):
            if r == k:
                continue
            factor = rows[r][k]
            for c in range(NV):
                if c == k:
                    rows[r][c] = -factor * pivot
                else:
                    rows[r][c] = rows[r][c] - factor * rows[k][c]
    return rows


def scalars(ref):
    return [[ref[r, c] for c in range(NV)] for r in range(NV)]


def steps(body, start, reverse=False):
    def several(t, carry):
        for u in range(STEP_UNROLL):
            i = t * STEP_UNROLL + u
            carry = body(STEPS - 1 - i if reverse else i, carry)
        return carry

    return lax.fori_loop(0, STEPS // STEP_UNROLL, several, start)


def far_first(count, me, body):
    def some(t, carry):
        for u in range(SEND_UNROLL // 2):
            d = t * (SEND_UNROLL // 2) + u
            body(lax.rem(me + count // 2 + d, count))
            body(lax.rem(me + count // 2 + count - 1 - d, count))
        return carry

    lax.fori_loop(0, count // SEND_UNROLL, some, 0)


def each(count, body):
    def one(k, carry):
        body(k)
        return carry

    lax.fori_loop(0, count, one, 0)


def kernel(
    state, visc_in, cl_in, cu_in, nl_in, nu_in, vm_hbm, cp_hbm, cm_hbm, np_hbm, nm_hbm,
    out,
    vm_in, cp_in, cm_in, np_in, nm_in, mat_sem,
    field, visc, cl, cu, nl, nu, rhs, low, turned, low_t,
    edge, edge_in, w_own, l_own, u_own, w_all, l_all, u_all, x_out, y_out, x_in, y_in,
    power, k_circ, k_norm, level, r_circ, a_low, a_up, g_low, g_up, m_norm, w_norm, rn, bn,
    load_sem, tl_sem, tu_sem,
    halo_send, halo_recv, w_send, w_recv, l_send, l_recv, u_send, u_recv,
    x_send, x_recv, y_send, y_recv,
    rn_send, rn_recv, bl_send, bl_recv, bu_send, bu_recv,
):
    c, n, s = lax.axis_index("circ"), lax.axis_index("norm"), lax.axis_index("span")
    owner = lax.rem(c, 2) == 0
    row = c // 2
    zero = jnp.zeros((STEPS, LANES), jnp.float32)
    one = jnp.ones((STEPS, LANES), jnp.float32)

    def remote(src, dst, send, recv, to):
        return pltpu.make_async_remote_copy(
            src_ref=src, dst_ref=dst, send_sem=send, recv_sem=recv, device_id=to, device_id_type=MESH
        )

    barrier = pltpu.get_barrier_semaphore()

    def greet(to):
        @pl.when(jnp.logical_or(jnp.logical_or(owner, to == c), lax.rem(to, 2) == 0))
        def _():
            pl.semaphore_signal(barrier, inc=1, device_id=(to, n, 1 - s), device_id_type=MESH)

    for d in (1, CIRC - 1):
        pl.semaphore_signal(
            barrier, inc=1, device_id=(lax.rem(c + d, CIRC), n, s), device_id_type=MESH
        )
    for d in range(1, NORM):
        pl.semaphore_signal(
            barrier, inc=1, device_id=(c, lax.rem(n + d, NORM), s), device_id_type=MESH
        )
    each(CIRC, greet)

    inside = pltpu.make_async_copy(
        state, field.at[:, pl.ds(1, STEPS), pl.ds(0, STEPS)], load_sem.at[0]
    )
    loads = [
        pltpu.make_async_copy(src, dst, load_sem.at[1 + k])
        for k, (src, dst) in enumerate(((cl_in, cl), (cu_in, cu), (visc_in, visc)))
    ]
    mats = [
        pltpu.make_async_copy(src, dst, mat_sem.at[k])
        for k, (src, dst) in enumerate(
            zip((vm_hbm, cp_hbm, cm_hbm, np_hbm, nm_hbm), (vm_in, cp_in, cm_in, np_in, nm_in))
        )
    ]
    inside.start()
    for copy in mats + loads:
        copy.start()

    def turn(src, dst, sem, j):
        return pltpu.make_async_copy(src.at[:, j], dst.at[j], sem.at[0])

    def fetch(j):
        turn(nl_in, nl, tl_sem, j).start()
        turn(nu_in, nu, tu_sem, j).start()

    each(STEPS, fetch)

    inside.wait()
    lane = lax.broadcasted_iota(jnp.int32, (STEPS, LANES), 1)

    def slot(a, i):
        return (0, a * STEPS + i) if a < 4 else (1, i)

    def pack(i, packs):
        packs = list(packs)
        for a in range(NV):
            g, k = slot(a, i)
            mine = lax.rem(lane - 2 * k + 1 + LANES, LANES) <= 1
            moved = pltpu.roll(field[a, i + 1, pl.ds(0, STEPS)], 2 * k, axis=1)
            packs[g] = jnp.where(mine, moved, packs[g])
        return tuple(packs)

    packs = steps(pack, (zero, zero))
    for g in range(2):
        edge[g] = jnp.where(lane % 2 == 1, pltpu.roll(packs[g], 2, axis=1), packs[g])

    pl.semaphore_wait(barrier, jnp.where(owner, CIRC, OWNERS + 1) + 2 + NORM - 1)

    to_next = remote(
        field.at[:, STEPS, pl.ds(0, STEPS)], field.at[:, 0, pl.ds(0, STEPS)],
        halo_send.at[0], halo_recv.at[0], (lax.rem(c + 1, CIRC), n, s),
    )
    to_prev = remote(
        field.at[:, 1, pl.ds(0, STEPS)], field.at[:, STEPS + 1, pl.ds(0, STEPS)],
        halo_send.at[1], halo_recv.at[1], (lax.rem(c + CIRC - 1, CIRC), n, s),
    )
    to_side = remote(edge, edge_in, halo_send.at[2], halo_recv.at[2], (c, n, 1 - s))
    to_up = remote(
        field.at[:, pl.ds(1, STEPS), STEPS - 1], field.at[:, pl.ds(1, STEPS), 23],
        halo_send.at[3], halo_recv.at[3], (c, n + 1, s),
    )
    to_down = remote(
        field.at[:, pl.ds(1, STEPS), 0], field.at[:, pl.ds(1, STEPS), STEPS],
        halo_send.at[4], halo_recv.at[4], (c, n - 1, s),
    )
    has_up, has_down = n < NORM - 1, n > 0
    to_next.start()
    to_prev.start()
    to_side.start()
    pl.when(has_up)(to_up.start)
    pl.when(has_down)(to_down.start)

    def nothing_at(at):
        def fill(i, carry):
            for a in range(NV):
                field[a, i + 1, pl.ds(at, 1)] = jnp.zeros((1, LANES), jnp.float32)
            return carry

        steps(fill, 0)

    pl.when(jnp.logical_not(has_up))(lambda: nothing_at(STEPS))
    pl.when(jnp.logical_not(has_down))(lambda: nothing_at(23))

    for copy in loads:
        copy.wait()

    def circ_scales(i, carry):
        p, q = carry
        p = p * cl[i]
        w_own[2 + i] = q * p
        return p, q * cu[i]

    p, q = steps(circ_scales, (one, one))
    w_own[0] = p
    w_own[1] = q

    def hand_in(src, dst, send, recv):
        far_first(OWNERS, row, lambda j: remote(
            src.at[:, j], dst.at[:, place(c)], send.at[0], recv.at[0], (2 * j, n, 1 - s)
        ).start())

    def give_back(src, dst, send, recv):
        far_first(CIRC, c, lambda k: remote(
            src.at[:, place(k)], dst.at[:, row], send.at[0], recv.at[0], (k, n, 1 - s)
        ).start())

    def whole(src, dst, send, recv):
        out_of = remote(src, src, send.at[0], recv.at[0], (c, n, 1 - s))
        into = remote(dst, dst, send.at[0], recv.at[0], (c, n, 1 - s))
        return out_of.wait_send, into.wait_recv

    def collected(*which):
        whole(*which)[1]()

    w_way = (w_own, w_all, w_send, w_recv)
    l_way = (l_own, l_all, l_send, l_recv)
    u_way = (u_own, u_all, u_send, u_recv)
    x_way = (x_out, x_in, x_send, x_recv)
    y_way = (y_out, y_in, y_send, y_recv)
    hand_in(*w_way)

    for copy in mats:
        copy.wait()
    lane8 = lax.broadcasted_iota(jnp.int32, (8, LANES), 1)
    sub8 = lax.broadcasted_iota(jnp.int32, (8, LANES), 0)
    group = lane8 // 32
    base = []
    for r in range(NV):
        for k in range(NV):
            base.append(
                jnp.where(
                    group == 0,
                    cp_in[r, k],
                    jnp.where(group == 1, cm_in[r, k], jnp.where(group == 2, np_in[r, k], nm_in[r, k])),
                )
            )

    def square(t, mat):
        for e in range(NV * NV):
            power[t, e] = mat[e]
        return tuple(matmul(mat, mat))

    last = lax.fori_loop(0, 9, square, tuple(base))
    for e in range(NV * NV):
        power[9, e] = last[e]

    def kept(t):
        return [power[t, e] for e in range(NV * NV)]

    run = [
        jnp.where(sub8 % 2 == 1, base[e], 1.0 if e % (NV + 1) == 0 else 0.0) for e in range(NV * NV)
    ]
    for bit in (1, 2):
        more = matmul(run, kept(bit))
        run = [jnp.where((sub8 // (1 << bit)) % 2 == 1, more[e], run[e]) for e in range(NV * NV)]
    for half in range(2):
        if half == 1:
            run = matmul(run, kept(3))
        ahead = matmul(run, kept(0))
        both = matmul(run, [pltpu.roll(x, 32, axis=1) for x in ahead])
        for e in range(NV * NV):
            k_circ[e, pl.ds(8 * half, 8)] = jnp.broadcast_to(both[e][:, 32:33], (8, LANES))
            k_norm[e, pl.ds(8 * half, 8)] = jnp.broadcast_to(both[e][:, 96:97], (8, LANES))

    def spread(t, carry):
        for e in range(NV * NV):
            mat = power[4 + t, e]
            level[t, e] = jnp.broadcast_to(mat[:, 0:1], (8, LANES))
            level[6 + t, e] = jnp.broadcast_to(mat[:, 32:33], (8, LANES))
        return carry

    lax.fori_loop(0, 6, spread, 0)
    for e in range(NV * NV):
        m_norm[0, e] = jnp.broadcast_to(power[4, e][:, 64:65], (8, LANES))
        m_norm[1, e] = jnp.broadcast_to(power[4, e][:, 96:97], (8, LANES))

    def responses(weight, count, table, store):
        for v in range(count):
            w = [weight(i, v) for i in range(STEPS)]
            for e in range(NV * NV):
                total = w[0] * table[e, pl.ds(0, 1)]
                for i in range(1, STEPS):
                    total = total + w[i] * table[e, pl.ds(i, 1)]
                store(e, v, total)


    to_next.wait_recv()
    to_prev.wait_recv()
    to_side.wait_recv()
    pl.when(has_up)(to_down.wait_recv)
    pl.when(has_down)(to_up.wait_recv)

    vm, cp, cm = scalars(vm_in), scalars(cp_in), scalars(cm_in)

    def sweep_step(value, scale, mat, carry):
        moved = apply(mat, carry)
        return tuple(value[a] + scale * moved[a] for a in range(NV))

    def first_low(i, carry):
        lap = []
        for a in range(NV):
            tall = field[a, i + 1]
            mid = tall[:STEPS]
            wall = pltpu.roll(tall, 1, axis=0)[:STEPS] + pltpu.roll(tall, 23, axis=0)[:STEPS]
            g, k = slot(a, i)
            beyond = pltpu.roll(edge_in[g], LANES - 1 - 2 * k, axis=1)
            left = jnp.where(lane == 0, beyond, pltpu.roll(mid, 1, axis=1))
            right = jnp.where(lane == LANES - 1, beyond, pltpu.roll(mid, LANES - 1, axis=1))
            around = field[a, i, pl.ds(0, STEPS)] + field[a, i + 2, pl.ds(0, STEPS)]
            lap.append(around + (left + right) + wall - 6.0 * mid)
        mixed = apply(vm, lap)
        value = [visc[i] * x for x in mixed]
        for a in range(NV):
            rhs[a, i] = value[a]
        carry = sweep_step(value, cl[i], cp, carry)
        for a in range(NV):
            low[a, i] = carry[a]
        return carry

    zeros = (zero,) * NV
    end = steps(first_low, zeros)
    for a in range(NV):
        l_own[a] = end[a]
    hand_in(*l_way)

    def first_up(i, carry):
        return sweep_step([low[a, i] for a in range(NV)], cu[i], cm, carry)

    end = steps(first_up, zeros, reverse=True)
    for a in range(NV):
        u_own[a] = end[a]
    hand_in(*u_way)

    pltpu.make_async_copy(nl_in, nl, tl_sem.at[0]).wait()
    pltpu.make_async_copy(nu_in, nu, tu_sem.at[0]).wait()

    def norm_scales(j, carry):
        p, q = carry
        p = p * nl[j]
        w_norm[j] = q * p
        return p, q * nu[j]

    p, q = steps(norm_scales, (one, one))
    rn[n, 0] = p
    rn[n, 1] = q

    def keep_norm(e, v, total):
        rn[n, 2 + e, pl.ds(8 * v, 8)] = total

    responses(lambda j, v: w_norm[j, pl.ds(8 * v, 8)], 2, k_norm, keep_norm)

    def over_norm(d, buf, send, recv):
        to = lax.rem(n + d, NORM)
        return remote(buf.at[n], buf.at[n], send.at[d], recv.at[n], (c, to, s))

    def from_norm(d, buf, send, recv):
        k = lax.rem(n + d, NORM)
        return remote(buf.at[k], buf.at[k], send.at[d], recv.at[k], (c, k, s))

    for d in range(1, NORM):
        over_norm(d, rn, rn_send, rn_recv).start()

    def quad(ref, *at):
        return [ref[(*at, pl.ds(8 * v, 8))] for v in range(4)]

    def table(ref, *at):
        return [[ref[(*at, NV * r + k)] for k in range(NV)] for r in range(NV)]

    @pl.when(owner)
    def _():
        collected(*w_way)

        def keep_circ(e, v, total):
            r_circ[e, pl.ds(8 * v, 8)] = total

        responses(lambda i, v: w_all[2 + i, pl.ds(8 * v, 8)], 4, k_circ, keep_circ)
        for side, (store, inv) in enumerate(((a_low, g_low), (a_up, g_up))):
            scale = quad(w_all, side)
            for t in range(5):
                for v in range(4):
                    store[t, pl.ds(8 * v, 8)] = scale[v]
                beside = shifted(scale, 1 << t, side == 1)
                scale = [scale[v] * beside[v] for v in range(4)]
            solved = inverse(scale[0], table(level, 6 * side + 5))
            for r in range(NV):
                for k in range(NV):
                    inv[NV * r + k] = solved[r][k]

        def closed(shift, side, store, inv):
            for t in range(5):
                beside = [shifted(x, 1 << t, side == 1) for x in shift]
                scale = quad(store, t)
                mat = table(level, 6 * side + t)
                moved = [apply(mat, [beside[a][v] for a in range(NV)]) for v in range(4)]
                shift = [
                    [shift[a][v] + scale[v] * moved[v][a] for v in range(4)] for a in range(NV)
                ]
            mat = table(inv)
            solved = [apply(mat, [shift[a][v] for a in range(NV)]) for v in range(4)]
            return [shifted([solved[v][a] for v in range(4)], 1, side == 1) for a in range(NV)]

        collected(*l_way)
        enter = closed([quad(l_all, a) for a in range(NV)], 0, a_low, g_low)
        for a in range(NV):
            for v in range(4):
                x_out[a, pl.ds(8 * v, 8)] = enter[a][v]
        give_back(*x_way)
        collected(*u_way)
        shift = [quad(u_all, a) for a in range(NV)]
        for r in range(NV):
            for k in range(NV):
                response = quad(r_circ, NV * r + k)
                shift[r] = [shift[r][v] + response[v] * enter[k][v] for v in range(4)]
        enter = closed(shift, 1, a_up, g_up)
        for a in range(NV):
            for v in range(4):
                y_out[a, pl.ds(8 * v, 8)] = enter[a][v]
        give_back(*y_way)

    collected(*x_way)

    def second_low(i, carry):
        carry = sweep_step([rhs[a, i] for a in range(NV)], cl[i], cp, carry)
        for a in range(NV):
            low[a, i] = carry[a]
        return carry

    steps(second_low, tuple(x_in[a] for a in range(NV)))
    collected(*y_way)

    def second_up(i, carry):
        carry = sweep_step([low[a, i] for a in range(NV)], cu[i], cm, carry)
        for a in range(NV):
            turned[a, pl.ds(i, STEPS, stride=STEPS)] = carry[a]
        return carry

    steps(second_up, tuple(y_in[a] for a in range(NV)), reverse=True)

    nplus, nminus = scalars(np_in), scalars(nm_in)

    def across(j):
        return [turned[a, pl.ds(pl.multiple_of(j * STEPS, STEPS), STEPS)] for a in range(NV)]

    def norm_low(j, carry):
        carry = sweep_step(across(j), nl[j], nplus, carry)
        for a in range(NV):
            low_t[a, j] = carry[a]
        return carry

    def norm_up(j, carry):
        return sweep_step([low_t[a, j] for a in range(NV)], nu[j], nminus, carry)

    bl, bu = bn.at[0], bn.at[1]
    end = steps(norm_low, zeros)
    for a in range(NV):
        bn[0, n, a] = end[a]
    for d in range(1, NORM):
        @pl.when(n < NORM - 1)
        def _():
            over_norm(d, bl, bl_send, bl_recv).start()

    end = steps(norm_up, zeros, reverse=True)
    for a in range(NV):
        bn[1, n, a] = end[a]
    for d in range(1, NORM):
        @pl.when(lax.rem(n + d, NORM) < n)
        def _():
            over_norm(d, bu, bu_send, bu_recv).start()

    for d in range(1, NORM):
        k = lax.rem(n + d, NORM)
        from_norm(d, rn, rn_send, rn_recv).wait_recv()
        pl.when(k < NORM - 1)(from_norm(d, bl, bl_send, bl_recv).wait_recv)
        pl.when(k > n)(from_norm(d, bu, bu_send, bu_recv).wait_recv)

    def entering(v):
        half = pl.ds(8 * v, 8)
        plus, minus = table(m_norm, 0), table(m_norm, 1)
        x = {1: [bn[0, 0, a, half] for a in range(NV)]}
        for k in (1, 2):
            moved = apply(plus, x[k])
            x[k + 1] = [bn[0, k, a, half] + rn[k, 0, half] * moved[a] for a in range(NV)]
        y = {}
        for k in (3, 2, 1):
            value = [bn[1, k, a, half] for a in range(NV)]
            for r in range(NV):
                for a in range(NV):
                    value[r] = value[r] + rn[k, 2 + NV * r + a, half] * x[k][a]
            if k < 3:
                moved = apply(minus, y[k])
                value = [value[a] + rn[k, 1, half] * moved[a] for a in range(NV)]
            y[k - 1] = value
        none = jnp.zeros((8, LANES), jnp.float32)
        low_in, up_in = [none] * NV, [none] * NV
        for k in (1, 2, 3):
            low_in = [jnp.where(n == k, x[k][a], low_in[a]) for a in range(NV)]
            up_in = [jnp.where(n == k - 1, y[k - 1][a], up_in[a]) for a in range(NV)]
        return low_in, up_in

    halves = [entering(v) for v in range(2)]
    starts = [
        tuple(jnp.concatenate([halves[0][side][a], halves[1][side][a]], axis=0) for a in range(NV))
        for side in range(2)
    ]
    steps(norm_low, starts[0])

    def last_up(j, carry):
        carry = norm_up(j, carry)
        for a in range(NV):
            out[a, pl.ds(j, STEPS, stride=STEPS)] = carry[a]
        return carry

    steps(last_up, starts[1], reverse=True)

    to_next.wait_send()
    to_prev.wait_send()
    to_side.wait_send()
    pl.when(has_up)(to_up.wait_send)
    pl.when(has_down)(to_down.wait_send)

    for way in (w_way, l_way, u_way):
        whole(*way)[0]()

    @pl.when(owner)
    def _():
        for way in (x_way, y_way):
            whole(*way)[0]()

    for d in range(1, NORM):
        over_norm(d, rn, rn_send, rn_recv).wait_send()
        pl.when(n < NORM - 1)(over_norm(d, bl, bl_send, bl_recv).wait_send)
        pl.when(lax.rem(n + d, NORM) < n)(over_norm(d, bu, bu_send, bu_recv).wait_send)


def per_device(
    state, viscosity, visc_matrix, circ_lower_coef, circ_upper_coef, normal_lower_coef,
    normal_upper_coef, circ_plus, circ_minus, normal_plus, normal_minus,
):
    f32 = jnp.float32

    def vmem(*shape):
        return pltpu.VMEM(shape, f32)

    plane = (STEPS, LANES)
    block = (STEPS, STEPS, LANES)
    mats = NV * NV
    dma = pltpu.SemaphoreType.DMA
    scratch = [
        *[pltpu.SMEM((NV, NV), f32) for _ in range(5)], dma((5,)),
        vmem(NV, STEPS + 2, 24, LANES),
        *[vmem(*block) for _ in range(5)],
        vmem(NV, *block), vmem(NV, *block),
        vmem(NV, STEPS * STEPS, LANES), vmem(NV, *block),
        vmem(2, *plane), vmem(2, *plane),
        vmem(18, *plane), vmem(NV, *plane), vmem(NV, *plane),
        vmem(18, CIRC, LANES), vmem(NV, CIRC, LANES), vmem(NV, CIRC, LANES),
        vmem(NV, CIRC, LANES), vmem(NV, CIRC, LANES), vmem(NV, *plane), vmem(NV, *plane),
        vmem(10, mats, 8, LANES),
        vmem(mats, *plane), vmem(mats, *plane),
        vmem(12, mats, 8, LANES), vmem(mats, CIRC, LANES),
        vmem(5, CIRC, LANES), vmem(5, CIRC, LANES),
        vmem(mats, 8, LANES), vmem(mats, 8, LANES), vmem(2, mats, 8, LANES),
        vmem(*block), vmem(NORM, mats + 2, *plane), vmem(2, NORM, NV, *plane),
        dma((4,)), dma((1,)), dma((1,)),
        dma((5,)), dma((5,)),
        *[dma((1,)) for _ in range(10)],
        *[dma((NORM,)) for _ in range(6)],
    ]
    anywhere = pl.BlockSpec(memory_space=pltpu.HBM)
    flat = pl.pallas_call(
        kernel,
        out_shape=pltpu.VMEM((NV, STEPS * STEPS, LANES), f32),
        in_specs=[anywhere] * 11,
        out_specs=pl.BlockSpec(memory_space=pltpu.VMEM),
        scratch_shapes=scratch,
        compiler_params=pltpu.CompilerParams(
            collective_id=0, has_side_effects=True, vmem_limit_bytes=60 * 1024 * 1024
        ),
    )(
        state, viscosity, circ_lower_coef, circ_upper_coef, normal_lower_coef, normal_upper_coef,
        visc_matrix, circ_plus, circ_minus, normal_plus, normal_minus,
    )
    return flat.reshape(NV, STEPS, STEPS, LANES)


def solution(mesh):
    placed = (
        P(None, "circ", "norm", "span"),
        P("circ", "norm", "span"),
        P(),
        P("circ", "norm", "span"),
        P("circ", "norm", "span"),
        P("circ", "norm", "span"),
        P("circ", "norm", "span"),
        P(),
        P(),
        P(),
        P(),
    )
    return jax.shard_map(
        per_device,
        mesh=mesh,
        in_specs=placed,
        out_specs=P(None, "circ", "norm", "span"),
        check_vma=False,
    )
```

```python
import jax
import jax.numpy as jnp
from jax import lax
from jax.experimental import pallas as pl
from jax.experimental.pallas import tpu as pltpu
from jax.sharding import PartitionSpec as P

MESH = pl.DeviceIdType.MESH
NV = 5
CIRC, NORM = 32, 4
STEPS = 16
LANES = 128
OWNERS = 16
STEP_UNROLL = 16
SEND_UNROLL = 2


def place(seg):
    return lax.rem(seg, 4) * 8 + seg // 4


def shifted(groups, d, reverse):
    def turn(x, k):
        return pltpu.roll(x, 8 - k if reverse else k, axis=0)

    if d >= 4:
        return [turn(x, d // 4) for x in groups]
    if reverse:
        return [groups[v + d] if v + d < 4 else turn(groups[v + d - 4], 1) for v in range(4)]
    return [groups[v - d] if v >= d else turn(groups[v - d + 4], 1) for v in range(4)]


def total(terms):
    while len(terms) > 1:
        pairs = [x + y for x, y in zip(terms[::2], terms[1::2])]
        terms = pairs + terms[2 * len(pairs) :]
    return terms[0]


def apply(mat, vec, more=None):
    out = []
    for r in range(NV):
        terms = [mat[r][c] * vec[c] for c in range(NV)]
        out.append(total(terms if more is None else terms + [more[r]]))
    return out


def matmul(a, b):
    out = []
    for r in range(NV):
        for c in range(NV):
            out.append(total([a[NV * r + k] * b[NV * k + c] for k in range(NV)]))
    return out


def inverse(rows):
    rows = [list(row) for row in rows]
    for k in range(NV):
        pivot = 1.0 / rows[k][k]
        for c in range(NV):
            rows[k][c] = pivot if c == k else rows[k][c] * pivot
        for r in range(NV):
            if r == k:
                continue
            factor = rows[r][k]
            for c in range(NV):
                if c == k:
                    rows[r][c] = -factor * pivot
                else:
                    rows[r][c] = rows[r][c] - factor * rows[k][c]
    return rows


def scalars(ref):
    return [[ref[r, c] for c in range(NV)] for r in range(NV)]


def steps(body, start, reverse=False):
    def several(t, carry):
        for u in range(STEP_UNROLL):
            i = t * STEP_UNROLL + u
            carry = body(STEPS - 1 - i if reverse else i, carry)
        return carry

    return lax.fori_loop(0, STEPS // STEP_UNROLL, several, start)


def far_first(count, me, body):
    def some(t, carry):
        for u in range(SEND_UNROLL // 2):
            d = t * (SEND_UNROLL // 2) + u
            body(lax.rem(me + count // 2 + d, count))
            body(lax.rem(me + count // 2 + count - 1 - d, count))
        return carry

    lax.fori_loop(0, count // SEND_UNROLL, some, 0)


def each(count, body):
    def one(k, carry):
        body(k)
        return carry

    lax.fori_loop(0, count, one, 0)


def kernel(
    state, visc_in, cl_in, cu_in, nl_in, nu_in, vm_hbm, cp_hbm, cm_hbm, np_hbm, nm_hbm,
    out,
    vm_in, cp_in, cm_in, np_in, nm_in, mat_sem,
    field, visc, cl, cu, nl, nu, rhs, low, turned, low_t,
    edge, edge_in, before, after, wall_lo, wall_hi, wall_mix, side_mix, w_own, l_own, u_own, w_all, l_all, u_all, x_out, y_out, x_in, y_in,
    power, k_circ, k_norm, level, r_circ, a_low, a_up, g_low, g_up,
    m_norm, rs, wn, rn, bn,
    load_sem, tl_sem, tu_sem,
    halo_send, halo_recv, w_send, w_recv, l_send, l_recv, u_send, u_recv,
    x_send, x_recv, y_send, y_recv,
    rs_send, rs_recv, wn_send, wn_recv, bl_send, bl_recv, bu_send, bu_recv,
):
    c, n, s = lax.axis_index("circ"), lax.axis_index("norm"), lax.axis_index("span")
    owner = lax.rem(c, 2) == 0
    not_owner = lax.rem(c, 2) == 1
    row = c // 2
    zero = jnp.zeros((STEPS, LANES), jnp.float32)
    one = jnp.ones((STEPS, LANES), jnp.float32)

    def remote(src, dst, send, recv, to):
        return pltpu.make_async_remote_copy(
            src_ref=src, dst_ref=dst, send_sem=send, recv_sem=recv, device_id=to, device_id_type=MESH
        )

    barrier = pltpu.get_barrier_semaphore()

    def greet(*to):
        pl.semaphore_signal(barrier, inc=1, device_id=to, device_id_type=MESH)

    greet(c, n, 1 - s)
    greet(lax.rem(c + 1, CIRC), n, s)
    greet(lax.rem(c + CIRC - 1, CIRC), n, s)
    for d in range(1, NORM):
        greet(c, lax.rem(n + d, NORM), s)

    @pl.when(owner)
    def _():
        each(CIRC - 1, lambda d: greet(lax.rem(c + d + 1, CIRC), n, 1 - s))

    @pl.when(not_owner)
    def _():
        each(OWNERS, lambda j: greet(2 * j, n, 1 - s))

    inside = pltpu.make_async_copy(
        state, field.at[:, pl.ds(1, STEPS)], load_sem.at[0]
    )
    loads = [
        pltpu.make_async_copy(src, dst, load_sem.at[1 + k])
        for k, (src, dst) in enumerate(((cl_in, cl), (cu_in, cu), (visc_in, visc)))
    ]
    mats = [
        pltpu.make_async_copy(src, dst, mat_sem.at[k])
        for k, (src, dst) in enumerate(
            zip((vm_hbm, cp_hbm, cm_hbm, np_hbm, nm_hbm), (vm_in, cp_in, cm_in, np_in, nm_in))
        )
    ]
    inside.start()
    for copy in mats + loads:
        copy.start()

    def turn(src, dst, sem, j):
        return pltpu.make_async_copy(src.at[:, j], dst.at[j], sem.at[0])

    def fetch(j):
        turn(nl_in, nl, tl_sem, j).start()
        turn(nu_in, nu, tu_sem, j).start()

    each(STEPS, fetch)

    to_next = remote(
        field.at[:, STEPS], before, halo_send.at[3], halo_recv.at[3], (lax.rem(c + 1, CIRC), n, s)
    )
    to_prev = remote(
        field.at[:, 1], after, halo_send.at[4], halo_recv.at[4], (lax.rem(c + CIRC - 1, CIRC), n, s)
    )
    inside.wait()
    lane = lax.broadcasted_iota(jnp.int32, (STEPS, LANES), 1)

    def slot(a, i):
        return (0, a * STEPS + i) if a < 4 else (1, i)

    def pack(i, packs):
        packs = list(packs)
        for a in range(NV):
            g, k = slot(a, i)
            mine = lax.rem(lane - 2 * k + 1 + LANES, LANES) <= 1
            moved = pltpu.roll(field[a, i + 1], 2 * k, axis=1)
            packs[g] = jnp.where(mine, moved, packs[g])
        return tuple(packs)

    packs = steps(pack, (zero, zero))
    for g in range(2):
        edge[g] = jnp.where(lane % 2 == 1, pltpu.roll(packs[g], 2, axis=1), packs[g])

    pl.semaphore_wait(barrier, jnp.where(owner, CIRC, OWNERS + 1) + 2 + NORM - 1)

    to_side = remote(edge, edge_in, halo_send.at[0], halo_recv.at[0], (c, n, 1 - s))
    to_up = remote(
        field.at[:, pl.ds(1, STEPS), STEPS - 1], wall_lo, halo_send.at[1], halo_recv.at[1], (c, n + 1, s)
    )
    to_down = remote(
        field.at[:, pl.ds(1, STEPS), 0], wall_hi, halo_send.at[2], halo_recv.at[2], (c, n - 1, s)
    )
    has_up, has_down = n < NORM - 1, n > 0
    to_next.start()
    to_prev.start()
    to_side.start()
    pl.when(has_up)(to_up.start)
    pl.when(has_down)(to_down.start)

    def clear(ref):
        for a in range(NV):
            ref[a] = zero

    pl.when(n == NORM - 1)(lambda: clear(wall_hi))
    pl.when(n == 0)(lambda: clear(wall_lo))

    for copy in loads + mats:
        copy.wait()
    vm, cp, cm = scalars(vm_in), scalars(cp_in), scalars(cm_in)

    def circ_scales(i, carry):
        p, q = carry
        p = p * cl[i]
        w_own[2 + i] = q * p
        return p, q * cu[i]

    p, q = steps(circ_scales, (one, one))
    w_own[0] = p
    w_own[1] = q

    def hand_in(src, dst, send, recv):
        far_first(OWNERS, row, lambda j: remote(
            src.at[:, j], dst.at[:, place(c)], send.at[0], recv.at[0], (2 * j, n, 1 - s)
        ).start())

    def give_back(src, dst, send, recv):
        far_first(CIRC, c, lambda k: remote(
            src.at[:, place(k)], dst.at[:, row], send.at[0], recv.at[0], (k, n, 1 - s)
        ).start())

    def whole(src, dst, send, recv):
        out_of = remote(src, src, send.at[0], recv.at[0], (c, n, 1 - s))
        into = remote(dst, dst, send.at[0], recv.at[0], (c, n, 1 - s))
        return out_of.wait_send, into.wait_recv

    def collected(*which):
        whole(*which)[1]()

    w_way = (w_own, w_all, w_send, w_recv)
    l_way = (l_own, l_all, l_send, l_recv)
    u_way = (u_own, u_all, u_send, u_recv)
    x_way = (x_out, x_in, x_send, x_recv)
    y_way = (y_out, y_in, y_send, y_recv)
    hand_in(*w_way)

    pltpu.make_async_copy(nl_in, nl, tl_sem.at[0]).wait()
    pltpu.make_async_copy(nu_in, nu, tu_sem.at[0]).wait()

    def norm_scales(j, carry):
        p, q = carry
        p = p * nl[j]
        wn[n, 1 + j] = q * p
        return p, q * nu[j]

    p, q = steps(norm_scales, (one, one))
    rs[n] = p
    wn[n, 0] = q

    def over_norm(d, buf, send, recv):
        to = lax.rem(n + d, NORM)
        return remote(buf.at[n], buf.at[n], send.at[d], recv.at[n], (c, to, s))

    def from_norm(d, buf, send, recv):
        k = lax.rem(n + d, NORM)
        return remote(buf.at[k], buf.at[k], send.at[d], recv.at[k], (c, k, s))

    def scale_used(k):
        return jnp.logical_and(k > 0, k < NORM - 1)

    for d in range(1, NORM):
        pl.when(scale_used(n))(over_norm(d, rs, rs_send, rs_recv).start)
        pl.when(lax.rem(n + d, NORM) < n)(over_norm(d, wn, wn_send, wn_recv).start)

    sub = lax.broadcasted_iota(jnp.int32, (STEPS, LANES), 0)
    for a in range(NV):
        field[a, 0] = zero
        field[a, STEPS + 1] = zero

    def inner(i, carry):
        lap = []
        for a in range(NV):
            mid = field[a, i + 1]
            below = jnp.where(sub == 0, 0.0, pltpu.roll(mid, 1, axis=0))
            above = jnp.where(sub == STEPS - 1, 0.0, pltpu.roll(mid, STEPS - 1, axis=0))
            left = jnp.where(lane == 0, 0.0, pltpu.roll(mid, 1, axis=1))
            right = jnp.where(lane == LANES - 1, 0.0, pltpu.roll(mid, LANES - 1, axis=1))
            around = field[a, i] + field[a, i + 2]
            lap.append(around + (left + right) + (below + above) - 6.0 * mid)
        mixed = apply(vm, lap)
        for a in range(NV):
            rhs[a, i] = visc[i] * mixed[a]
        return carry

    steps(inner, 0)

    to_next.wait_recv()
    to_prev.wait_recv()
    to_side.wait_recv()
    pl.when(has_up)(to_down.wait_recv)
    pl.when(has_down)(to_up.wait_recv)

    for k, ref in enumerate((wall_lo, wall_hi)):
        mixed = apply(vm, [ref[a] for a in range(NV)])
        for a in range(NV):
            wall_mix[k, a] = mixed[a]
    mixed = apply(
        vm,
        [edge_in[0]]
        + [pltpu.roll(edge_in[0], LANES - 32 * a, axis=1) for a in range(1, 4)]
        + [edge_in[1]],
    )
    for a in range(NV):
        side_mix[a] = mixed[a]
    for at, ref in ((0, before), (STEPS - 1, after)):
        mixed = apply(vm, [ref[a] for a in range(NV)])
        for a in range(NV):
            rhs[a, at] = rhs[a, at] + visc[at] * mixed[a]
    lane_half = lax.broadcasted_iota(jnp.int32, (8, LANES), 1)
    sub_half = lax.broadcasted_iota(jnp.int32, (8, LANES), 0)
    outer = jnp.logical_or(lane_half == 0, lane_half == LANES - 1)

    def sweep_step(value, scale, mat, carry):
        return tuple(apply(mat, [scale * x for x in carry], value))

    def first_low(i, carry):
        value = []
        for a in range(NV):
            beyond = pltpu.roll(side_mix[a], LANES - 1 - 2 * i, axis=1)
            more = []
            for h in range(2):
                wall = jnp.where(sub_half == 7 * h, wall_mix[h, a, pl.ds(i, 1)], 0.0)
                more.append(jnp.where(outer, beyond[8 * h : 8 * h + 8], 0.0) + wall)
            value.append(rhs[a, i] + visc[i] * jnp.concatenate(more, axis=0))
            rhs[a, i] = value[a]
        carry = sweep_step(value, cl[i], cp, carry)
        for a in range(NV):
            low[a, i] = carry[a]
        return carry

    zeros = (zero,) * NV
    end = steps(first_low, zeros)
    for a in range(NV):
        l_own[a] = end[a]
    hand_in(*l_way)

    def first_up(i, carry):
        return sweep_step([low[a, i] for a in range(NV)], cu[i], cm, carry)

    end = steps(first_up, zeros, reverse=True)
    for a in range(NV):
        u_own[a] = end[a]
    hand_in(*u_way)

    lane8 = lax.broadcasted_iota(jnp.int32, (8, LANES), 1)
    sub8 = lax.broadcasted_iota(jnp.int32, (8, LANES), 0)
    group = lane8 // 32
    base = []
    for r in range(NV):
        for k in range(NV):
            base.append(
                jnp.where(
                    group == 0,
                    cp_in[r, k],
                    jnp.where(group == 1, cm_in[r, k], jnp.where(group == 2, np_in[r, k], nm_in[r, k])),
                )
            )

    def square(t, mat):
        for e in range(NV * NV):
            power[t, e] = mat[e]
        return tuple(matmul(mat, mat))

    last = lax.fori_loop(0, 9, square, tuple(base))
    for e in range(NV * NV):
        power[9, e] = last[e]

    def kept(t):
        return [power[t, e] for e in range(NV * NV)]

    run = [
        jnp.where(sub8 % 2 == 1, base[e], 1.0 if e % (NV + 1) == 0 else 0.0) for e in range(NV * NV)
    ]
    for bit in (1, 2):
        more = matmul(run, kept(bit))
        run = [jnp.where((sub8 // (1 << bit)) % 2 == 1, more[e], run[e]) for e in range(NV * NV)]
    for half in range(2):
        if half == 1:
            run = matmul(run, kept(3))
        ahead = matmul(run, kept(0))
        both = matmul(run, [pltpu.roll(x, 32, axis=1) for x in ahead])
        for e in range(NV * NV):
            k_circ[e, pl.ds(8 * half, 8)] = jnp.broadcast_to(both[e][:, 32:33], (8, LANES))
            k_norm[e, pl.ds(8 * half, 8)] = jnp.broadcast_to(both[e][:, 96:97], (8, LANES))

    def spread(t, carry):
        for e in range(NV * NV):
            mat = power[4 + t, e]
            level[t, e] = jnp.broadcast_to(mat[:, 0:1], (8, LANES))
            level[6 + t, e] = jnp.broadcast_to(mat[:, 32:33], (8, LANES))
        return carry

    lax.fori_loop(0, 6, spread, 0)
    for e in range(NV * NV):
        m_norm[0, e] = jnp.broadcast_to(power[4, e][:, 64:65], (8, LANES))
        m_norm[1, e] = jnp.broadcast_to(power[4, e][:, 96:97], (8, LANES))

    def responses(weight, count, table, store):
        for v in range(count):
            w = [weight(i, v) for i in range(STEPS)]
            for e in range(NV * NV):
                store(e, v, total([w[i] * table[e, pl.ds(i, 1)] for i in range(STEPS)]))


    def quad(ref, *at):
        return [ref[(*at, pl.ds(8 * v, 8))] for v in range(4)]

    def table(ref, *at):
        return [[ref[(*at, NV * r + k)] for k in range(NV)] for r in range(NV)]

    @pl.when(owner)
    def _():
        collected(*w_way)

        def keep_circ(e, v, total):
            r_circ[e, pl.ds(8 * v, 8)] = total

        responses(lambda i, v: w_all[2 + i, pl.ds(8 * v, 8)], 4, k_circ, keep_circ)
        for side, (store, inv) in enumerate(((a_low, g_low), (a_up, g_up))):
            scale = quad(w_all, side)
            for t in range(5):
                for v in range(4):
                    store[t, pl.ds(8 * v, 8)] = scale[v]
                beside = shifted(scale, 1 << t, side == 1)
                scale = [scale[v] * beside[v] for v in range(4)]
            whole_turn = table(level, 6 * side + 5)
            solved = inverse([
                [(1.0 if r == k else 0.0) - scale[0] * whole_turn[r][k] for k in range(NV)]
                for r in range(NV)
            ])
            for r in range(NV):
                for k in range(NV):
                    inv[NV * r + k] = solved[r][k]

        def closed(shift, side, store, inv):
            for t in range(5):
                beside = [shifted(x, 1 << t, side == 1) for x in shift]
                scale = quad(store, t)
                mat = table(level, 6 * side + t)
                moved = [
                    apply(
                        mat,
                        [scale[v] * beside[a][v] for a in range(NV)],
                        [shift[a][v] for a in range(NV)],
                    )
                    for v in range(4)
                ]
                shift = [[moved[v][a] for v in range(4)] for a in range(NV)]
            mat = table(inv)
            solved = [apply(mat, [shift[a][v] for a in range(NV)]) for v in range(4)]
            return [shifted([solved[v][a] for v in range(4)], 1, side == 1) for a in range(NV)]

        collected(*l_way)
        enter = closed([quad(l_all, a) for a in range(NV)], 0, a_low, g_low)
        for a in range(NV):
            for v in range(4):
                x_out[a, pl.ds(8 * v, 8)] = enter[a][v]
        give_back(*x_way)
        collected(*u_way)
        shift = [quad(u_all, a) for a in range(NV)]
        for r in range(NV):
            for k in range(NV):
                response = quad(r_circ, NV * r + k)
                shift[r] = [shift[r][v] + response[v] * enter[k][v] for v in range(4)]
        enter = closed(shift, 1, a_up, g_up)
        for a in range(NV):
            for v in range(4):
                y_out[a, pl.ds(8 * v, 8)] = enter[a][v]
        give_back(*y_way)

    for d in range(1, NORM):
        k = lax.rem(n + d, NORM)
        pl.when(k > n)(from_norm(d, wn, wn_send, wn_recv).wait_recv)

    def of_norm(k):
        def keep_norm(e, v, total):
            rn[k, e, pl.ds(8 * v, 8)] = total

        @pl.when(k > n)
        def _():
            responses(lambda j, v: wn[k, 1 + j, pl.ds(8 * v, 8)], 2, k_norm, keep_norm)

    each(NORM, of_norm)
    for d in range(1, NORM):
        k = lax.rem(n + d, NORM)
        pl.when(scale_used(k))(from_norm(d, rs, rs_send, rs_recv).wait_recv)
    plus_16, minus_16 = table(m_norm, 0), table(m_norm, 1)

    def product(a, b):
        return [
            [total([a[r][k] * b[k][c] for k in range(NV)]) for c in range(NV)] for r in range(NV)
        ]

    def fold(k):
        for v in range(2):
            half = pl.ds(8 * v, 8)
            beyond = [[rn[k + 1, NV * r + c, half] for c in range(NV)] for r in range(NV)]
            moved = product(minus_16, [[wn[k, 0, half] * x for x in line] for line in beyond])

            @pl.when(k == n)
            def _():
                for r in range(NV):
                    for c in range(NV):
                        rn[k, NV * r + c, half] = moved[r][c]

            @pl.when(k > n)
            def _():
                both = product(moved, plus_16)
                for r in range(NV):
                    for c in range(NV):
                        rn[k, NV * r + c, half] = rn[k, NV * r + c, half] + rs[k, half] * both[r][c]

    for k in (2, 1):
        pl.when(k >= n)(lambda k=k: fold(k))

    collected(*x_way)

    def second_low(i, carry):
        carry = sweep_step([rhs[a, i] for a in range(NV)], cl[i], cp, carry)
        for a in range(NV):
            low[a, i] = carry[a]
        return carry

    steps(second_low, tuple(x_in[a] for a in range(NV)))
    collected(*y_way)

    def second_up(i, carry):
        carry = sweep_step([low[a, i] for a in range(NV)], cu[i], cm, carry)
        for a in range(NV):
            turned[a, pl.ds(i, STEPS, stride=STEPS)] = carry[a]
        return carry

    steps(second_up, tuple(y_in[a] for a in range(NV)), reverse=True)

    nplus, nminus = scalars(np_in), scalars(nm_in)

    def across(j):
        return [turned[a, pl.ds(pl.multiple_of(j * STEPS, STEPS), STEPS)] for a in range(NV)]

    def norm_low(j, carry):
        carry = sweep_step(across(j), nl[j], nplus, carry)
        for a in range(NV):
            low_t[a, j] = carry[a]
        return carry

    def norm_up(j, carry):
        return sweep_step([low_t[a, j] for a in range(NV)], nu[j], nminus, carry)

    bl, bu = bn.at[0], bn.at[1]
    end = steps(norm_low, zeros)
    for a in range(NV):
        bn[0, n, a] = end[a]
    for d in range(1, NORM):
        pl.when(lax.rem(n + d, NORM) > n)(over_norm(d, bl, bl_send, bl_recv).start)

    below = end
    end = steps(norm_up, zeros, reverse=True)
    for v in range(2):
        half = pl.ds(8 * v, 8)
        own = [[rn[n, NV * r + a, half] for a in range(NV)] for r in range(NV)]
        added = apply(own, [x[8 * v : 8 * v + 8] for x in below])
        for a in range(NV):
            upper = end[a][8 * v : 8 * v + 8]
            bn[1, n, a, half] = upper + jnp.where(scale_used(n), added[a], 0.0)
    for d in range(1, NORM):
        pl.when(lax.rem(n + d, NORM) < n)(over_norm(d, bu, bu_send, bu_recv).start)

    for d in range(1, NORM):
        k = lax.rem(n + d, NORM)
        pl.when(k < n)(from_norm(d, bl, bl_send, bl_recv).wait_recv)

    none = jnp.zeros((8, LANES), jnp.float32)

    def joined(halves):
        return tuple(
            jnp.concatenate([halves[0][a], halves[1][a]], axis=0) for a in range(NV)
        )

    def chosen(by_place):
        enter = [none] * NV
        for k, value in by_place.items():
            enter = [jnp.where(n == k, value[a], enter[a]) for a in range(NV)]
        return enter

    def entering_low(v):
        half = pl.ds(8 * v, 8)
        x = {1: [bn[0, 0, a, half] for a in range(NV)]}
        for k in (1, 2):
            x[k + 1] = apply(
                plus_16, [rs[k, half] * y for y in x[k]], [bn[0, k, a, half] for a in range(NV)]
            )
        return chosen(x)

    start = joined([entering_low(v) for v in range(2)])
    leave = steps(norm_low, start)

    for d in range(1, NORM):
        k = lax.rem(n + d, NORM)
        pl.when(k > n)(from_norm(d, bu, bu_send, bu_recv).wait_recv)

    after_me = lax.rem(n + 1, NORM)

    def entering_up(v):
        half = pl.ds(8 * v, 8)
        y = {2: [bn[1, 3, a, half] for a in range(NV)]}
        for k in (2, 1):
            y[k - 1] = apply(
                minus_16, [wn[k, 0, half] * z for z in y[k]], [bn[1, k, a, half] for a in range(NV)]
            )
        mat = [[rn[after_me, NV * r + a, half] for a in range(NV)] for r in range(NV)]
        enter = apply(mat, [x[8 * v : 8 * v + 8] for x in leave], chosen(y))
        return [jnp.where(n < NORM - 1, x, 0.0) for x in enter]

    start = joined([entering_up(v) for v in range(2)])

    def last_up(j, carry):
        carry = norm_up(j, carry)
        for a in range(NV):
            out[a, pl.ds(j, STEPS, stride=STEPS)] = carry[a]
        return carry

    steps(last_up, start, reverse=True)

    to_next.wait_send()
    to_prev.wait_send()
    to_side.wait_send()
    pl.when(has_up)(to_up.wait_send)
    pl.when(has_down)(to_down.wait_send)

    for way in (w_way, l_way, u_way):
        whole(*way)[0]()

    @pl.when(owner)
    def _():
        for way in (x_way, y_way):
            whole(*way)[0]()

    for d in range(1, NORM):
        pl.when(scale_used(n))(over_norm(d, rs, rs_send, rs_recv).wait_send)
        pl.when(lax.rem(n + d, NORM) < n)(over_norm(d, wn, wn_send, wn_recv).wait_send)
        pl.when(lax.rem(n + d, NORM) > n)(over_norm(d, bl, bl_send, bl_recv).wait_send)
        pl.when(lax.rem(n + d, NORM) < n)(over_norm(d, bu, bu_send, bu_recv).wait_send)


def per_device(
    state, viscosity, visc_matrix, circ_lower_coef, circ_upper_coef, normal_lower_coef,
    normal_upper_coef, circ_plus, circ_minus, normal_plus, normal_minus,
):
    f32 = jnp.float32

    def vmem(*shape):
        return pltpu.VMEM(shape, f32)

    plane = (STEPS, LANES)
    block = (STEPS, STEPS, LANES)
    mats = NV * NV
    dma = pltpu.SemaphoreType.DMA
    scratch = [
        *[pltpu.SMEM((NV, NV), f32) for _ in range(5)], dma((5,)),
        vmem(NV, STEPS + 2, *plane),
        *[vmem(*block) for _ in range(5)],
        vmem(NV, *block), vmem(NV, *block),
        vmem(NV, STEPS * STEPS, LANES), vmem(NV, *block),
        vmem(2, *plane), vmem(2, *plane),
        vmem(NV, *plane), vmem(NV, *plane),
        vmem(NV, *plane), vmem(NV, *plane), vmem(2, NV, *plane), vmem(NV, *plane),
        vmem(18, *plane), vmem(NV, *plane), vmem(NV, *plane),
        vmem(18, CIRC, LANES), vmem(NV, CIRC, LANES), vmem(NV, CIRC, LANES),
        vmem(NV, CIRC, LANES), vmem(NV, CIRC, LANES), vmem(NV, *plane), vmem(NV, *plane),
        vmem(10, mats, 8, LANES),
        vmem(mats, *plane), vmem(mats, *plane),
        vmem(12, mats, 8, LANES), vmem(mats, CIRC, LANES),
        vmem(5, CIRC, LANES), vmem(5, CIRC, LANES),
        vmem(mats, 8, LANES), vmem(mats, 8, LANES),
        vmem(2, mats, 8, LANES), vmem(NORM, *plane), vmem(NORM, 1 + STEPS, *plane),
        vmem(NORM, mats, *plane), vmem(2, NORM, NV, *plane),
        dma((4,)), dma((1,)), dma((1,)),
        dma((5,)), dma((5,)),
        *[dma((1,)) for _ in range(10)],
        *[dma((NORM,)) for _ in range(8)],
    ]
    anywhere = pl.BlockSpec(memory_space=pltpu.HBM)
    flat = pl.pallas_call(
        kernel,
        out_shape=pltpu.VMEM((NV, STEPS * STEPS, LANES), f32),
        in_specs=[anywhere] * 11,
        out_specs=pl.BlockSpec(memory_space=pltpu.VMEM),
        scratch_shapes=scratch,
        compiler_params=pltpu.CompilerParams(
            collective_id=0, has_side_effects=True, vmem_limit_bytes=60 * 1024 * 1024
        ),
    )(
        state, viscosity, circ_lower_coef, circ_upper_coef, normal_lower_coef, normal_upper_coef,
        visc_matrix, circ_plus, circ_minus, normal_plus, normal_minus,
    )
    return flat.reshape(NV, STEPS, STEPS, LANES)


def solution(mesh):
    placed = (
        P(None, "circ", "norm", "span"),
        P("circ", "norm", "span"),
        P(),
        P("circ", "norm", "span"),
        P("circ", "norm", "span"),
        P("circ", "norm", "span"),
        P("circ", "norm", "span"),
        P(),
        P(),
        P(),
        P(),
    )
    return jax.shard_map(
        per_device,
        mesh=mesh,
        in_specs=placed,
        out_specs=P(None, "circ", "norm", "span"),
        check_vma=False,
    )
```

```python
import jax
import jax.numpy as jnp
from jax import lax
from jax.experimental import pallas as pl
from jax.experimental.pallas import tpu as pltpu
from jax.sharding import PartitionSpec as P

MESH = pl.DeviceIdType.MESH
NV = 5
CIRC, NORM = 32, 4
STEPS = 16
LANES = 128
OWNERS = 16
STEP_UNROLL = 16
SEND_UNROLL = 4


def place(seg):
    return lax.rem(seg, 4) * 8 + seg // 4


def shifted(groups, d, reverse):
    def turn(x, k):
        return pltpu.roll(x, 8 - k if reverse else k, axis=0)

    if d >= 4:
        return [turn(x, d // 4) for x in groups]
    if reverse:
        return [groups[v + d] if v + d < 4 else turn(groups[v + d - 4], 1) for v in range(4)]
    return [groups[v - d] if v >= d else turn(groups[v - d + 4], 1) for v in range(4)]


def total(terms):
    while len(terms) > 1:
        pairs = [x + y for x, y in zip(terms[::2], terms[1::2])]
        terms = pairs + terms[2 * len(pairs) :]
    return terms[0]


def apply(mat, vec, more=None):
    out = []
    for r in range(NV):
        terms = [mat[r][c] * vec[c] for c in range(NV)]
        out.append(total(terms if more is None else terms + [more[r]]))
    return out


def matmul(a, b):
    out = []
    for r in range(NV):
        for c in range(NV):
            out.append(total([a[NV * r + k] * b[NV * k + c] for k in range(NV)]))
    return out


def inverse(rows):
    rows = [list(row) for row in rows]
    for k in range(NV):
        pivot = 1.0 / rows[k][k]
        for c in range(NV):
            rows[k][c] = pivot if c == k else rows[k][c] * pivot
        for r in range(NV):
            if r == k:
                continue
            factor = rows[r][k]
            for c in range(NV):
                if c == k:
                    rows[r][c] = -factor * pivot
                else:
                    rows[r][c] = rows[r][c] - factor * rows[k][c]
    return rows


def scalars(ref):
    return [[ref[r, c] for c in range(NV)] for r in range(NV)]


def steps(body, start, reverse=False):
    def several(t, carry):
        for u in range(STEP_UNROLL):
            i = t * STEP_UNROLL + u
            carry = body(STEPS - 1 - i if reverse else i, carry)
        return carry

    return lax.fori_loop(0, STEPS // STEP_UNROLL, several, start)


def far_first(count, me, body):
    def some(t, carry):
        for u in range(SEND_UNROLL // 2):
            d = t * (SEND_UNROLL // 2) + u
            body(lax.rem(me + count // 2 + d, count))
            body(lax.rem(me + count // 2 + count - 1 - d, count))
        return carry

    lax.fori_loop(0, count // SEND_UNROLL, some, 0)


def each(count, body):
    def one(k, carry):
        body(k)
        return carry

    lax.fori_loop(0, count, one, 0)


def kernel(
    state, visc_in, cl_in, cu_in, nl_in, nu_in, vm_hbm, cp_hbm, cm_hbm, np_hbm, nm_hbm,
    out,
    vm_in, cp_in, cm_in, np_in, nm_in, mat_sem,
    field, visc, cl, cu, nl, nu, rhs, low, turned, low_t,
    edge, edge_in, before, after, wall_lo, wall_hi, wall_mix, side_mix, w_own, l_own, u_own, w_all, l_all, u_all, x_out, y_out, x_in, y_in,
    power, k_circ, k_norm, level, r_circ, a_low, a_up, g_low, g_up,
    m_norm, rs, wn, rn, bn,
    load_sem, tl_sem, tu_sem,
    halo_send, halo_recv, w_send, w_recv, l_send, l_recv, u_send, u_recv,
    x_send, x_recv, y_send, y_recv,
    rs_send, rs_recv, wn_send, wn_recv, bl_send, bl_recv, bu_send, bu_recv,
):
    c, n, s = lax.axis_index("circ"), lax.axis_index("norm"), lax.axis_index("span")
    owner = lax.rem(c, 2) == 0
    not_owner = lax.rem(c, 2) == 1
    row = c // 2
    zero = jnp.zeros((STEPS, LANES), jnp.float32)
    one = jnp.ones((STEPS, LANES), jnp.float32)

    def remote(src, dst, send, recv, to):
        return pltpu.make_async_remote_copy(
            src_ref=src, dst_ref=dst, send_sem=send, recv_sem=recv, device_id=to, device_id_type=MESH
        )

    barrier = pltpu.get_barrier_semaphore()

    def greet(*to):
        pl.semaphore_signal(barrier, inc=1, device_id=to, device_id_type=MESH)

    greet(c, n, 1 - s)
    greet(lax.rem(c + 1, CIRC), n, s)
    greet(lax.rem(c + CIRC - 1, CIRC), n, s)
    for d in range(1, NORM):
        greet(c, lax.rem(n + d, NORM), s)

    @pl.when(owner)
    def _():
        each(CIRC - 1, lambda d: greet(lax.rem(c + d + 1, CIRC), n, 1 - s))

    @pl.when(not_owner)
    def _():
        each(OWNERS, lambda j: greet(2 * j, n, 1 - s))

    inside = pltpu.make_async_copy(
        state, field.at[:, pl.ds(1, STEPS)], load_sem.at[0]
    )
    loads = [
        pltpu.make_async_copy(src, dst, load_sem.at[1 + k])
        for k, (src, dst) in enumerate(((cl_in, cl), (cu_in, cu), (visc_in, visc)))
    ]
    mats = [
        pltpu.make_async_copy(src, dst, mat_sem.at[k])
        for k, (src, dst) in enumerate(
            zip((vm_hbm, cp_hbm, cm_hbm, np_hbm, nm_hbm), (vm_in, cp_in, cm_in, np_in, nm_in))
        )
    ]
    inside.start()
    for copy in mats + loads:
        copy.start()

    def turn(src, dst, sem, j):
        return pltpu.make_async_copy(src.at[:, j], dst.at[j], sem.at[0])

    def fetch(j):
        turn(nl_in, nl, tl_sem, j).start()
        turn(nu_in, nu, tu_sem, j).start()

    each(STEPS, fetch)

    to_next = remote(
        field.at[:, STEPS], before, halo_send.at[3], halo_recv.at[3], (lax.rem(c + 1, CIRC), n, s)
    )
    to_prev = remote(
        field.at[:, 1], after, halo_send.at[4], halo_recv.at[4], (lax.rem(c + CIRC - 1, CIRC), n, s)
    )
    inside.wait()
    lane = lax.broadcasted_iota(jnp.int32, (STEPS, LANES), 1)

    def slot(a, i):
        return (0, a * STEPS + i) if a < 4 else (1, i)

    def pack(i, packs):
        packs = list(packs)
        for a in range(NV):
            g, k = slot(a, i)
            mine = lax.rem(lane - 2 * k + 1 + LANES, LANES) <= 1
            moved = pltpu.roll(field[a, i + 1], 2 * k, axis=1)
            packs[g] = jnp.where(mine, moved, packs[g])
        return tuple(packs)

    packs = steps(pack, (zero, zero))
    for g in range(2):
        edge[g] = jnp.where(lane % 2 == 1, pltpu.roll(packs[g], 2, axis=1), packs[g])

    pl.semaphore_wait(barrier, jnp.where(owner, CIRC, OWNERS + 1) + 2 + NORM - 1)

    to_side = remote(edge, edge_in, halo_send.at[0], halo_recv.at[0], (c, n, 1 - s))
    to_up = remote(
        field.at[:, pl.ds(1, STEPS), STEPS - 1], wall_lo, halo_send.at[1], halo_recv.at[1], (c, n + 1, s)
    )
    to_down = remote(
        field.at[:, pl.ds(1, STEPS), 0], wall_hi, halo_send.at[2], halo_recv.at[2], (c, n - 1, s)
    )
    has_up, has_down = n < NORM - 1, n > 0
    to_next.start()
    to_prev.start()
    to_side.start()
    pl.when(has_up)(to_up.start)
    pl.when(has_down)(to_down.start)

    def clear(ref):
        for a in range(NV):
            ref[a] = zero

    pl.when(n == NORM - 1)(lambda: clear(wall_hi))
    pl.when(n == 0)(lambda: clear(wall_lo))

    for copy in loads + mats:
        copy.wait()
    vm, cp, cm = scalars(vm_in), scalars(cp_in), scalars(cm_in)

    def circ_scales(i, carry):
        p, q = carry
        p = p * cl[i]
        w_own[2 + i] = q * p
        return p, q * cu[i]

    p, q = steps(circ_scales, (one, one))
    w_own[0] = p
    w_own[1] = q

    def hand_in(src, dst, send, recv):
        far_first(OWNERS, row, lambda j: remote(
            src.at[:, j], dst.at[:, place(c)], send.at[0], recv.at[0], (2 * j, n, 1 - s)
        ).start())

    def give_back(src, dst, send, recv):
        far_first(CIRC, c, lambda k: remote(
            src.at[:, place(k)], dst.at[:, row], send.at[0], recv.at[0], (k, n, 1 - s)
        ).start())

    def whole(src, dst, send, recv):
        out_of = remote(src, src, send.at[0], recv.at[0], (c, n, 1 - s))
        into = remote(dst, dst, send.at[0], recv.at[0], (c, n, 1 - s))
        return out_of.wait_send, into.wait_recv

    def collected(*which):
        whole(*which)[1]()

    w_way = (w_own, w_all, w_send, w_recv)
    l_way = (l_own, l_all, l_send, l_recv)
    u_way = (u_own, u_all, u_send, u_recv)
    x_way = (x_out, x_in, x_send, x_recv)
    y_way = (y_out, y_in, y_send, y_recv)
    hand_in(*w_way)

    pltpu.make_async_copy(nl_in, nl, tl_sem.at[0]).wait()
    pltpu.make_async_copy(nu_in, nu, tu_sem.at[0]).wait()

    def norm_scales(j, carry):
        p, q = carry
        p = p * nl[j]
        wn[n, 1 + j] = q * p
        return p, q * nu[j]

    p, q = steps(norm_scales, (one, one))
    rs[n] = p
    wn[n, 0] = q

    def over_norm(d, buf, send, recv):
        to = lax.rem(n + d, NORM)
        return remote(buf.at[n], buf.at[n], send.at[d], recv.at[n], (c, to, s))

    def from_norm(d, buf, send, recv):
        k = lax.rem(n + d, NORM)
        return remote(buf.at[k], buf.at[k], send.at[d], recv.at[k], (c, k, s))

    def scale_used(k):
        return jnp.logical_and(k > 0, k < NORM - 1)

    for d in range(1, NORM):
        pl.when(scale_used(n))(over_norm(d, rs, rs_send, rs_recv).start)
        pl.when(lax.rem(n + d, NORM) < n)(over_norm(d, wn, wn_send, wn_recv).start)

    sub = lax.broadcasted_iota(jnp.int32, (STEPS, LANES), 0)
    for a in range(NV):
        field[a, 0] = zero
        field[a, STEPS + 1] = zero

    def inner(i, carry):
        lap = []
        for a in range(NV):
            mid = field[a, i + 1]
            below = jnp.where(sub == 0, 0.0, pltpu.roll(mid, 1, axis=0))
            above = jnp.where(sub == STEPS - 1, 0.0, pltpu.roll(mid, STEPS - 1, axis=0))
            left = jnp.where(lane == 0, 0.0, pltpu.roll(mid, 1, axis=1))
            right = jnp.where(lane == LANES - 1, 0.0, pltpu.roll(mid, LANES - 1, axis=1))
            around = field[a, i] + field[a, i + 2]
            lap.append(around + (left + right) + (below + above) - 6.0 * mid)
        mixed = apply(vm, lap)
        for a in range(NV):
            rhs[a, i] = visc[i] * mixed[a]
        return carry

    steps(inner, 0)

    to_next.wait_recv()
    to_prev.wait_recv()
    to_side.wait_recv()
    pl.when(has_up)(to_down.wait_recv)
    pl.when(has_down)(to_up.wait_recv)

    for k, ref in enumerate((wall_lo, wall_hi)):
        mixed = apply(vm, [ref[a] for a in range(NV)])
        for a in range(NV):
            wall_mix[k, a] = mixed[a]
    mixed = apply(
        vm,
        [edge_in[0]]
        + [pltpu.roll(edge_in[0], LANES - 32 * a, axis=1) for a in range(1, 4)]
        + [edge_in[1]],
    )
    for a in range(NV):
        side_mix[a] = mixed[a]
    for at, ref in ((0, before), (STEPS - 1, after)):
        mixed = apply(vm, [ref[a] for a in range(NV)])
        for a in range(NV):
            rhs[a, at] = rhs[a, at] + visc[at] * mixed[a]
    lane_half = lax.broadcasted_iota(jnp.int32, (8, LANES), 1)
    sub_half = lax.broadcasted_iota(jnp.int32, (8, LANES), 0)
    outer = jnp.logical_or(lane_half == 0, lane_half == LANES - 1)

    def sweep_step(value, scale, mat, carry):
        return tuple(apply(mat, [scale * x for x in carry], value))

    def first_low(i, carry):
        value = []
        for a in range(NV):
            beyond = pltpu.roll(side_mix[a], LANES - 1 - 2 * i, axis=1)
            more = []
            for h in range(2):
                wall = jnp.where(sub_half == 7 * h, wall_mix[h, a, pl.ds(i, 1)], 0.0)
                more.append(jnp.where(outer, beyond[8 * h : 8 * h + 8], 0.0) + wall)
            value.append(rhs[a, i] + visc[i] * jnp.concatenate(more, axis=0))
            rhs[a, i] = value[a]
        carry = sweep_step(value, cl[i], cp, carry)
        for a in range(NV):
            low[a, i] = carry[a]
        return carry

    zeros = (zero,) * NV
    end = steps(first_low, zeros)
    for a in range(NV):
        l_own[a] = end[a]
    hand_in(*l_way)

    def first_up(i, carry):
        return sweep_step([low[a, i] for a in range(NV)], cu[i], cm, carry)

    end = steps(first_up, zeros, reverse=True)
    for a in range(NV):
        u_own[a] = end[a]
    hand_in(*u_way)

    lane8 = lax.broadcasted_iota(jnp.int32, (8, LANES), 1)
    sub8 = lax.broadcasted_iota(jnp.int32, (8, LANES), 0)
    group = lane8 // 32
    base = []
    for r in range(NV):
        for k in range(NV):
            base.append(
                jnp.where(
                    group == 0,
                    cp_in[r, k],
                    jnp.where(group == 1, cm_in[r, k], jnp.where(group == 2, np_in[r, k], nm_in[r, k])),
                )
            )

    def square(t, mat):
        for e in range(NV * NV):
            power[t, e] = mat[e]
        return tuple(matmul(mat, mat))

    last = lax.fori_loop(0, 9, square, tuple(base))
    for e in range(NV * NV):
        power[9, e] = last[e]

    def kept(t):
        return [power[t, e] for e in range(NV * NV)]

    run = [
        jnp.where(sub8 % 2 == 1, base[e], 1.0 if e % (NV + 1) == 0 else 0.0) for e in range(NV * NV)
    ]
    for bit in (1, 2):
        more = matmul(run, kept(bit))
        run = [jnp.where((sub8 // (1 << bit)) % 2 == 1, more[e], run[e]) for e in range(NV * NV)]
    for half in range(2):
        if half == 1:
            run = matmul(run, kept(3))
        ahead = matmul(run, kept(0))
        both = matmul(run, [pltpu.roll(x, 32, axis=1) for x in ahead])
        for e in range(NV * NV):
            k_circ[e, pl.ds(8 * half, 8)] = jnp.broadcast_to(both[e][:, 32:33], (8, LANES))
            k_norm[e, pl.ds(8 * half, 8)] = jnp.broadcast_to(both[e][:, 96:97], (8, LANES))

    def spread(t, carry):
        for e in range(NV * NV):
            mat = power[4 + t, e]
            level[t, e] = jnp.broadcast_to(mat[:, 0:1], (8, LANES))
            level[6 + t, e] = jnp.broadcast_to(mat[:, 32:33], (8, LANES))
        return carry

    lax.fori_loop(0, 6, spread, 0)
    for e in range(NV * NV):
        m_norm[0, e] = jnp.broadcast_to(power[4, e][:, 64:65], (8, LANES))
        m_norm[1, e] = jnp.broadcast_to(power[4, e][:, 96:97], (8, LANES))

    def responses(weight, count, table, store):
        for v in range(count):
            w = [weight(i, v) for i in range(STEPS)]
            for e in range(NV * NV):
                store(e, v, total([w[i] * table[e, pl.ds(i, 1)] for i in range(STEPS)]))


    def quad(ref, *at):
        return [ref[(*at, pl.ds(8 * v, 8))] for v in range(4)]

    def table(ref, *at):
        return [[ref[(*at, NV * r + k)] for k in range(NV)] for r in range(NV)]

    @pl.when(owner)
    def _():
        collected(*w_way)

        def keep_circ(e, v, total):
            r_circ[e, pl.ds(8 * v, 8)] = total

        responses(lambda i, v: w_all[2 + i, pl.ds(8 * v, 8)], 4, k_circ, keep_circ)
        for side, (store, inv) in enumerate(((a_low, g_low), (a_up, g_up))):
            scale = quad(w_all, side)
            for t in range(5):
                for v in range(4):
                    store[t, pl.ds(8 * v, 8)] = scale[v]
                beside = shifted(scale, 1 << t, side == 1)
                scale = [scale[v] * beside[v] for v in range(4)]
            whole_turn = table(level, 6 * side + 5)
            solved = inverse([
                [(1.0 if r == k else 0.0) - scale[0] * whole_turn[r][k] for k in range(NV)]
                for r in range(NV)
            ])
            for r in range(NV):
                for k in range(NV):
                    inv[NV * r + k] = solved[r][k]

        def closed(shift, side, store, inv):
            for t in range(5):
                beside = [shifted(x, 1 << t, side == 1) for x in shift]
                scale = quad(store, t)
                mat = table(level, 6 * side + t)
                moved = [
                    apply(
                        mat,
                        [scale[v] * beside[a][v] for a in range(NV)],
                        [shift[a][v] for a in range(NV)],
                    )
                    for v in range(4)
                ]
                shift = [[moved[v][a] for v in range(4)] for a in range(NV)]
            mat = table(inv)
            solved = [apply(mat, [shift[a][v] for a in range(NV)]) for v in range(4)]
            return [shifted([solved[v][a] for v in range(4)], 1, side == 1) for a in range(NV)]

        collected(*l_way)
        enter = closed([quad(l_all, a) for a in range(NV)], 0, a_low, g_low)
        for a in range(NV):
            for v in range(4):
                x_out[a, pl.ds(8 * v, 8)] = enter[a][v]
        give_back(*x_way)
        collected(*u_way)
        shift = [quad(u_all, a) for a in range(NV)]
        for r in range(NV):
            for k in range(NV):
                response = quad(r_circ, NV * r + k)
                shift[r] = [shift[r][v] + response[v] * enter[k][v] for v in range(4)]
        enter = closed(shift, 1, a_up, g_up)
        for a in range(NV):
            for v in range(4):
                y_out[a, pl.ds(8 * v, 8)] = enter[a][v]
        give_back(*y_way)

    for d in range(1, NORM):
        k = lax.rem(n + d, NORM)
        pl.when(k > n)(from_norm(d, wn, wn_send, wn_recv).wait_recv)

    def of_norm(k):
        def keep_norm(e, v, total):
            rn[k, e, pl.ds(8 * v, 8)] = total

        @pl.when(k > n)
        def _():
            responses(lambda j, v: wn[k, 1 + j, pl.ds(8 * v, 8)], 2, k_norm, keep_norm)

    each(NORM, of_norm)
    for d in range(1, NORM):
        k = lax.rem(n + d, NORM)
        pl.when(scale_used(k))(from_norm(d, rs, rs_send, rs_recv).wait_recv)
    plus_16, minus_16 = table(m_norm, 0), table(m_norm, 1)

    def product(a, b):
        return [
            [total([a[r][k] * b[k][c] for k in range(NV)]) for c in range(NV)] for r in range(NV)
        ]

    def fold(k):
        for v in range(2):
            half = pl.ds(8 * v, 8)
            beyond = [[rn[k + 1, NV * r + c, half] for c in range(NV)] for r in range(NV)]
            moved = product(minus_16, [[wn[k, 0, half] * x for x in line] for line in beyond])

            @pl.when(k == n)
            def _():
                for r in range(NV):
                    for c in range(NV):
                        rn[k, NV * r + c, half] = moved[r][c]

            @pl.when(k > n)
            def _():
                both = product(moved, plus_16)
                for r in range(NV):
                    for c in range(NV):
                        rn[k, NV * r + c, half] = rn[k, NV * r + c, half] + rs[k, half] * both[r][c]

    for k in (2, 1):
        pl.when(k >= n)(lambda k=k: fold(k))

    collected(*x_way)

    def second_low(i, carry):
        carry = sweep_step([rhs[a, i] for a in range(NV)], cl[i], cp, carry)
        for a in range(NV):
            low[a, i] = carry[a]
        return carry

    steps(second_low, tuple(x_in[a] for a in range(NV)))
    collected(*y_way)

    def second_up(i, carry):
        carry = sweep_step([low[a, i] for a in range(NV)], cu[i], cm, carry)
        for a in range(NV):
            turned[a, pl.ds(i, STEPS, stride=STEPS)] = carry[a]
        return carry

    steps(second_up, tuple(y_in[a] for a in range(NV)), reverse=True)

    nplus, nminus = scalars(np_in), scalars(nm_in)

    def across(j):
        return [turned[a, pl.ds(pl.multiple_of(j * STEPS, STEPS), STEPS)] for a in range(NV)]

    def norm_low(j, carry):
        carry = sweep_step(across(j), nl[j], nplus, carry)
        for a in range(NV):
            low_t[a, j] = carry[a]
        return carry

    def norm_up(j, carry):
        return sweep_step([low_t[a, j] for a in range(NV)], nu[j], nminus, carry)

    bl, bu = bn.at[0], bn.at[1]
    end = steps(norm_low, zeros)
    for a in range(NV):
        bn[0, n, a] = end[a]
    for d in range(1, NORM):
        pl.when(lax.rem(n + d, NORM) > n)(over_norm(d, bl, bl_send, bl_recv).start)

    below = end
    end = steps(norm_up, zeros, reverse=True)
    for v in range(2):
        half = pl.ds(8 * v, 8)
        own = [[rn[n, NV * r + a, half] for a in range(NV)] for r in range(NV)]
        added = apply(own, [x[8 * v : 8 * v + 8] for x in below])
        for a in range(NV):
            upper = end[a][8 * v : 8 * v + 8]
            bn[1, n, a, half] = upper + jnp.where(scale_used(n), added[a], 0.0)
    for d in range(1, NORM):
        pl.when(lax.rem(n + d, NORM) < n)(over_norm(d, bu, bu_send, bu_recv).start)

    to_next.wait_send()
    to_prev.wait_send()
    to_side.wait_send()
    pl.when(has_up)(to_up.wait_send)
    pl.when(has_down)(to_down.wait_send)

    for way in (w_way, l_way, u_way):
        whole(*way)[0]()

    @pl.when(owner)
    def _():
        for way in (x_way, y_way):
            whole(*way)[0]()

    for d in range(1, NORM):
        pl.when(scale_used(n))(over_norm(d, rs, rs_send, rs_recv).wait_send)
        pl.when(lax.rem(n + d, NORM) < n)(over_norm(d, wn, wn_send, wn_recv).wait_send)

    for d in range(1, NORM):
        k = lax.rem(n + d, NORM)
        pl.when(k < n)(from_norm(d, bl, bl_send, bl_recv).wait_recv)

    none = jnp.zeros((8, LANES), jnp.float32)

    def joined(halves):
        return tuple(
            jnp.concatenate([halves[0][a], halves[1][a]], axis=0) for a in range(NV)
        )

    def chosen(by_place):
        enter = [none] * NV
        for k, value in by_place.items():
            enter = [jnp.where(n == k, value[a], enter[a]) for a in range(NV)]
        return enter

    def entering_low(v):
        half = pl.ds(8 * v, 8)
        x = {1: [bn[0, 0, a, half] for a in range(NV)]}
        for k in (1, 2):
            x[k + 1] = apply(
                plus_16, [rs[k, half] * y for y in x[k]], [bn[0, k, a, half] for a in range(NV)]
            )
        return chosen(x)

    start = joined([entering_low(v) for v in range(2)])
    leave = steps(norm_low, start)

    for d in range(1, NORM):
        k = lax.rem(n + d, NORM)
        pl.when(k > n)(from_norm(d, bu, bu_send, bu_recv).wait_recv)

    after_me = lax.rem(n + 1, NORM)

    def entering_up(v):
        half = pl.ds(8 * v, 8)
        y = {2: [bn[1, 3, a, half] for a in range(NV)]}
        for k in (2, 1):
            y[k - 1] = apply(
                minus_16, [wn[k, 0, half] * z for z in y[k]], [bn[1, k, a, half] for a in range(NV)]
            )
        mat = [[rn[after_me, NV * r + a, half] for a in range(NV)] for r in range(NV)]
        enter = apply(mat, [x[8 * v : 8 * v + 8] for x in leave], chosen(y))
        return [jnp.where(n < NORM - 1, x, 0.0) for x in enter]

    start = joined([entering_up(v) for v in range(2)])

    def last_up(j, carry):
        carry = norm_up(j, carry)
        for a in range(NV):
            out[a, pl.ds(j, STEPS, stride=STEPS)] = carry[a]
        return carry

    steps(last_up, start, reverse=True)

    for d in range(1, NORM):
        pl.when(lax.rem(n + d, NORM) > n)(over_norm(d, bl, bl_send, bl_recv).wait_send)
        pl.when(lax.rem(n + d, NORM) < n)(over_norm(d, bu, bu_send, bu_recv).wait_send)


def per_device(
    state, viscosity, visc_matrix, circ_lower_coef, circ_upper_coef, normal_lower_coef,
    normal_upper_coef, circ_plus, circ_minus, normal_plus, normal_minus,
):
    f32 = jnp.float32

    def vmem(*shape):
        return pltpu.VMEM(shape, f32)

    plane = (STEPS, LANES)
    block = (STEPS, STEPS, LANES)
    mats = NV * NV
    dma = pltpu.SemaphoreType.DMA
    scratch = [
        *[pltpu.SMEM((NV, NV), f32) for _ in range(5)], dma((5,)),
        vmem(NV, STEPS + 2, *plane),
        *[vmem(*block) for _ in range(5)],
        vmem(NV, *block), vmem(NV, *block),
        vmem(NV, STEPS * STEPS, LANES), vmem(NV, *block),
        vmem(2, *plane), vmem(2, *plane),
        vmem(NV, *plane), vmem(NV, *plane),
        vmem(NV, *plane), vmem(NV, *plane), vmem(2, NV, *plane), vmem(NV, *plane),
        vmem(18, *plane), vmem(NV, *plane), vmem(NV, *plane),
        vmem(18, CIRC, LANES), vmem(NV, CIRC, LANES), vmem(NV, CIRC, LANES),
        vmem(NV, CIRC, LANES), vmem(NV, CIRC, LANES), vmem(NV, *plane), vmem(NV, *plane),
        vmem(10, mats, 8, LANES),
        vmem(mats, *plane), vmem(mats, *plane),
        vmem(12, mats, 8, LANES), vmem(mats, CIRC, LANES),
        vmem(5, CIRC, LANES), vmem(5, CIRC, LANES),
        vmem(mats, 8, LANES), vmem(mats, 8, LANES),
        vmem(2, mats, 8, LANES), vmem(NORM, *plane), vmem(NORM, 1 + STEPS, *plane),
        vmem(NORM, mats, *plane), vmem(2, NORM, NV, *plane),
        dma((4,)), dma((1,)), dma((1,)),
        dma((5,)), dma((5,)),
        *[dma((1,)) for _ in range(10)],
        *[dma((NORM,)) for _ in range(8)],
    ]
    anywhere = pl.BlockSpec(memory_space=pltpu.HBM)
    flat = pl.pallas_call(
        kernel,
        out_shape=pltpu.VMEM((NV, STEPS * STEPS, LANES), f32),
        in_specs=[anywhere] * 11,
        out_specs=pl.BlockSpec(memory_space=pltpu.VMEM),
        scratch_shapes=scratch,
        compiler_params=pltpu.CompilerParams(
            collective_id=0, has_side_effects=True, vmem_limit_bytes=60 * 1024 * 1024
        ),
    )(
        state, viscosity, circ_lower_coef, circ_upper_coef, normal_lower_coef, normal_upper_coef,
        visc_matrix, circ_plus, circ_minus, normal_plus, normal_minus,
    )
    return flat.reshape(NV, STEPS, STEPS, LANES)


def solution(mesh):
    placed = (
        P(None, "circ", "norm", "span"),
        P("circ", "norm", "span"),
        P(),
        P("circ", "norm", "span"),
        P("circ", "norm", "span"),
        P("circ", "norm", "span"),
        P("circ", "norm", "span"),
        P(),
        P(),
        P(),
        P(),
    )
    return jax.shard_map(
        per_device,
        mesh=mesh,
        in_specs=placed,
        out_specs=P(None, "circ", "norm", "span"),
        check_vma=False,
    )
```
